512 devices in a mesh: dp: 2 (over z_hi), row: 32 (over z_lo, y), col: 8 (over x, core).
Axes of the slice: x: 4, y: 4, z: 16 (z_hi: 2, z_lo: 8; z = z_hi * 8 + z_lo), core: 2. Of those that a mesh axis runs over, the one named last changes fastest.
Arguments:
- finals: bfloat16 [2048, 4096], P('dp', 'col'), may hold values from -16 to 16
- head_weight: bfloat16 [16384, 4096], P('row', 'col'), may hold values from -0.234375 to 0.234375
- hidden: bfloat16 [2048, 10240], P('dp', 'row'), may hold values from -6 to 6
- targets: int32 [2048], P('dp'), may hold values from 0 to 16383
- head_rows_old: float32 [16384], P('row'), may hold values from 1e-06 to 0.09
- head_cols_old: float32 [4096], P('col'), may hold values from 0.00025 to 0.0075
- down_rows_old: float32 [10240], P('row'), may hold values from 0.05 to 3
- down_cols_old: float32 [4096], P('col'), may hold values from 0.05 to 1.5
Outputs:
- head_update: float32 [16384, 4096], P('row', 'col')
- head_rows: float32 [16384], P('row')
- head_cols: float32 [4096], P('col')
- down_update: float32 [10240, 4096], P('row', 'col')
- down_rows: float32 [10240], P('row')
- down_cols: float32 [4096], P('col')
The draws below stay inside these ranges and needn't reach their ends.
All inputs are finite; a program needn't handle non-finite values.
Results may differ from the reference program's by a relative error of at most 0.003.
Values may be sent and summed in bfloat16 or wider, within the bound.
A program may use at most 64 MiB of HBM per device.

```python
import math
import jax
import jax.numpy as jnp
import numpy as np
from jax import lax

D = 4096
FF = 10240
VOCAB = 16384
TOKENS = 2048


def shared_weight(key):
    values = jax.random.normal(key, (VOCAB, D), jnp.float32) * (3.0 / math.sqrt(D))
    return jnp.clip(values, -0.234375, 0.234375)


def ramped_levels(key, length, lowest, highest):
    spread = jax.random.uniform(key, (length,), jnp.float32)
    levels = jnp.exp(math.log(lowest) + spread * (math.log(highest) - math.log(lowest)))
    ramp_up = 1.0 + 2.0 * jnp.arange(length, dtype=jnp.float32) / max(length - 1, 1)
    return levels * ramp_up


def draw_head_weight(key, part):
    return shared_weight(key).astype(jnp.bfloat16)


def draw_finals(key, part):
    key = jax.random.fold_in(key, 11)
    values = jnp.clip(jax.random.normal(jax.random.fold_in(key, 1), (TOKENS, D), jnp.float32), -6.0, 6.0)
    return jnp.clip(values, -16.0, 16.0).astype(jnp.bfloat16)


def draw_head_rows_old(key, part):
    key = jax.random.fold_in(key, 21)
    return ramped_levels(key, VOCAB, 1e-06, 0.03)


def draw_head_cols_old(key, part):
    key = jax.random.fold_in(key, 22)
    return ramped_levels(key, D, 0.00025, 0.0025)


def draw_down_rows_old(key, part):
    key = jax.random.fold_in(key, 23)
    return ramped_levels(key, FF, 0.05, 1.0)


def draw_down_cols_old(key, part):
    key = jax.random.fold_in(key, 24)
    return ramped_levels(key, D, 0.05, 0.5)


def touch_ends(entries, stream_key, smallest, largest):
    extent = entries.shape
    index_at = [jax.random.randint(jax.random.fold_in(stream_key, axis), (), 0, extent[axis]) for axis in range(len(extent))]
    entries = entries.at[tuple(index_at)].set(smallest)
    longest = extent.index(max(extent))
    index_at[longest] = (index_at[longest] + 1) % extent[longest]
    return entries.at[tuple(index_at)].set(largest)


def steps_of(own_key, extent, split, least, largest):
    factor_of = 1.0
    for axis_at, shards_of in split:
        draws = jax.random.uniform(jax.random.fold_in(jax.random.fold_in(own_key, 6), axis_at), (shards_of,), jnp.float32, least / len(split), largest / len(split))
        factor_of = factor_of * jnp.repeat(jnp.exp(draws), extent[axis_at] // shards_of).reshape((-1,) + (1,) * (len(extent) - 1 - axis_at))
    return factor_of


def rank_bounds(number_of, lean):
    loads = [(1 << 20) // math.isqrt(rank ** lean) + 1 for rank in range(1, number_of + 1)]
    scale = 1 + sum(loads) // (1 << 30)
    return np.cumsum(np.array([max(1, weight // scale) for weight in loads]))


def skewed_ids(own_key, shape, count, skew):
    listing = rank_bounds(count, skew)
    lot = jax.random.randint(jax.random.fold_in(own_key, 1), shape, 0, int(listing[count - 1]))
    standing = jnp.searchsorted(jnp.asarray(listing, jnp.int32), lot, side="right")
    return jax.random.permutation(jax.random.fold_in(own_key, 2), count)[standing].astype(jnp.int32)


def bell_draw(rng, shape, width, reach, split=(), held_as=jnp.bfloat16):
    entries = width * jax.random.normal(rng, shape, jnp.float32)
    if split:
        entries = entries * steps_of(rng, shape, split, -0.22, 0.18)
    return jnp.clip(entries, -reach, reach).astype(held_as)


def setup_inputs(seed: int = 0) -> dict:
    splits = jax.random.split(jax.random.key(seed), 9)
    return {
        "finals": draw_finals(jax.random.fold_in(splits[8], 71), 0),
        "head_weight": draw_head_weight(jax.random.fold_in(splits[8], 71), 0),
        "hidden": bell_draw(splits[2], (TOKENS, FF), 1.0, 6.0, ((0, 2), (1, 32))),
        "targets": touch_ends(skewed_ids(splits[3], (TOKENS,), VOCAB, 2), jax.random.fold_in(splits[3], 3), 0, VOCAB - 1).astype(jnp.int32),
        "head_rows_old": draw_head_rows_old(jax.random.fold_in(splits[8], 71), 0),
        "head_cols_old": draw_head_cols_old(jax.random.fold_in(splits[8], 71), 0),
        "down_rows_old": draw_down_rows_old(jax.random.fold_in(splits[8], 71), 0),
        "down_cols_old": draw_down_cols_old(jax.random.fold_in(splits[8], 71), 0),
    }


EPS_SQUARE = 1e-30
DECAY_RATE = 1.0 - 10.0 ** (-0.8)
CLIP_LEVEL = 1.0

def factored(gradient, rows_old, cols_old):
    squares = gradient * gradient + EPS_SQUARE
    rows_new = DECAY_RATE * rows_old + (1.0 - DECAY_RATE) * lax.optimization_barrier(jnp.mean(squares, axis=1))
    cols_new = DECAY_RATE * cols_old + (1.0 - DECAY_RATE) * lax.optimization_barrier(jnp.mean(squares, axis=0))
    raw_update = gradient / jnp.sqrt(rows_new[:, None] * cols_new[None, :])
    rms_ratio = jnp.sqrt(jnp.mean(raw_update * raw_update)) / CLIP_LEVEL
    return (raw_update / jnp.maximum(1.0, rms_ratio), rows_new, cols_new)

def reference(finals, head_weight, hidden, targets, head_rows_old, head_cols_old, down_rows_old, down_cols_old):
    logits = jnp.dot(finals, head_weight.T, preferred_element_type=jnp.float32)
    row_max = lax.optimization_barrier(jnp.max(logits, axis=1, keepdims=True))
    shifted = jnp.exp(logits - row_max)
    row_sum = lax.optimization_barrier(jnp.sum(shifted, axis=1, keepdims=True))
    vocab_ids = jnp.arange(VOCAB, dtype=jnp.int32)
    onehot = (targets[:, None] == vocab_ids[None, :]).astype(jnp.float32)
    dlogits = (shifted / row_sum - onehot).astype(jnp.bfloat16)
    head_grad = jnp.dot(dlogits.T, finals, preferred_element_type=jnp.float32)
    dfinals = jnp.dot(dlogits, head_weight, preferred_element_type=jnp.float32).astype(jnp.bfloat16)
    down_grad = jnp.dot(hidden.T, dfinals, preferred_element_type=jnp.float32)
    head_update, head_rows, head_cols = factored(head_grad, head_rows_old, head_cols_old)
    down_update, down_rows, down_cols = factored(down_grad, down_rows_old, down_cols_old)
    return (head_update, head_rows, head_cols, down_update, down_rows, down_cols)
```

```python
import jax
import jax.numpy as jnp
from jax import lax
from jax.experimental import pallas as pl
from jax.experimental.pallas import tpu as pltpu
from jax.sharding import PartitionSpec as P

EPS_SQUARE = 1e-30
DECAY_RATE = 1.0 - 10.0 ** (-0.8)
CLIP_LEVEL = 1.0
F32, BF16, I16 = jnp.float32, jnp.bfloat16, jnp.int16
MESH = pl.DeviceIdType.MESH

NZ, NY, NX = 8, 4, 4
T = 1024
V = 512
D = 512
FF = 320
C = 128
FULL_V, FULL_D, FULL_FF = 16384, 4096, 10240
QD = D // NY
BD = QD // NZ
LIMIT = 32766.0


def tokens_dot(left, right):
    return lax.dot_general(left, right, (((1,), (1,)), ((), ())), preferred_element_type=F32)


def plain_dot(left, right):
    return jnp.dot(left, right, preferred_element_type=F32)


def unit_of(values):
    peak = jnp.max(jnp.abs(values), axis=0, keepdims=True)
    return jnp.maximum(peak, 1e-30) * (1.0 / LIMIT)


def coded(values, unit):
    return jnp.round(values * (1.0 / unit)).astype(jnp.int32).astype(I16)


def decoded(codes, unit):
    return codes.astype(jnp.int32).astype(F32) * unit


def lanes_to_tile(ref, row, vector):
    for part in range(vector.shape[1] // 128):
        ref[pl.ds(row + part, 1), :] = vector[:, 128 * part : 128 * part + 128]


def tile_to_lanes(tile, row, parts):
    return jnp.concatenate([tile[row + p : row + p + 1, :] for p in range(parts)], axis=1)


def column_to_lanes(column):
    return jnp.broadcast_to(column, (column.shape[0], 128)).T[0:1, :]


def lanes_to_column(vector):
    return jnp.broadcast_to(vector, (128, vector.shape[1])).T[:, 0:1]


def body(
    fin_in, w_in, hid_in, tgt, hro, hco, dro, dco,
    hup, hrows, hcols, dup, drows, dcols,
    fin, w, wt, hid, hidt, dl,
    part, core_out, core_in, x_out, x_in, xu_out, xu_in,
    stat, dft, y_out, y_in, yu_out, yu_in, z_out, z_in, zu_out, zu_in,
    dfb, hg, dg, rtile, ctile, ztile, stile,
    local_sem, send_sem, recv_sem,
):
    d, row, col = lax.axis_index("dp"), lax.axis_index("row"), lax.axis_index("col")
    z, y, x, k = row // NY, row % NY, col // 2, col % 2
    zz = d * NZ + z
    od = 1 - d

    def at(dd, z_, y_, c_):
        return (dd, z_ * NY + y_, c_)

    def ring(o):
        q = (zz + o) % (2 * NZ)
        return at(q // NZ, q % NZ, y, col)

    def x_peer(o):
        return (d, row, ((x + o) % NX) * 2 + k)

    def y_peer(o):
        return at(d, z, (y + o) % NY, col)

    def z_peer(o):
        return at(d, (z + o) % NZ, y, col)

    core = (d, row, 2 * x + 1 - k)
    dp_peer = (od, row, col)
    mirror = at(od, NZ - 1 - z, y, col)

    pending = []
    count = [0]

    def remote(src, dst, device, slot=None):
        if slot is None:
            slot = count[0]
            count[0] += 1
        copy = pltpu.make_async_remote_copy(
            src_ref=src, dst_ref=dst, send_sem=send_sem.at[slot], recv_sem=recv_sem.at[slot],
            device_id=device, device_id_type=MESH,
        )
        copy.start()
        pending.append(copy)
        return copy

    loads = [
        pltpu.make_async_copy(fin_in, fin.at[pl.ds(d * T, T), :], local_sem.at[0]),
        pltpu.make_async_copy(w_in, w, local_sem.at[1]),
        pltpu.make_async_copy(hid_in, hid.at[pl.ds(d * T, T), :], local_sem.at[2]),
    ]
    for load in loads:
        load.start()

    barrier = pltpu.get_barrier_semaphore()

    def greet(device):
        pl.semaphore_signal(barrier, inc=1, device_id=device, device_id_type=MESH)

    @pl.loop(1, 32)
    def _(o):
        greet((d, (row + o) % 32, col))

    @pl.loop(1, 8)
    def _(o):
        greet((d, row, (col + o) % 8))

    others = [dp_peer, mirror] + [ring(o) for o in (1, -1, 2, -2, 4, -4)]
    for device in others:
        greet(device)
    pl.semaphore_wait(barrier, 31 + 7 + len(others))
    for load in loads:
        load.wait()

    fq = pl.multiple_of(d * T + (y * NZ + z) * 32, 32)
    fin_cross = remote(fin.at[pl.ds(fq, 32), :], fin.at[pl.ds(fq, 32), :], mirror)
    hq = pl.multiple_of(d * T + col * C, C)
    hid_cross = remote(hid.at[pl.ds(hq, C), :], hid.at[pl.ds(hq, C), :], dp_peer)

    def logits_part(c):
        start = pl.multiple_of(d * T + c * C, C)
        return tokens_dot(w[...], fin[pl.ds(start, C), :])

    core_copies = {}
    for o in (1, 2, 3, 0):
        xo = (x + o) % NX
        core_out[o] = logits_part(2 * xo + 1 - k)
        core_copies[o] = remote(core_out.at[o], core_in.at[o], core)
    for o in (1, 2, 3, 0):
        xo = (x + o) % NX
        part[o] = logits_part(2 * xo + k)
    x_copies = []
    for o in (1, 2, 3):
        core_copies[o].wait_recv()
        total = part[o] + core_in[o]
        unit = unit_of(total)
        x_out[o - 1] = coded(total, unit)
        xu_out[o - 1] = unit
        x_copies.append(remote(x_out.at[o - 1], x_in.at[o - 1], x_peer(o)))
        x_copies.append(remote(xu_out.at[o - 1], xu_in.at[o - 1], x_peer(o)))
    core_copies[0].wait_recv()
    part[0] = part[0] + core_in[0]
    wt[...] = w[...].T

    fin_cross.wait_recv()
    gq = pl.multiple_of(od * T + (y * NZ + NZ - 1 - z) * 32, 32)
    fin_z = [
        remote(fin.at[pl.ds(gq, 32), :], fin.at[pl.ds(gq, 32), :], z_peer(o)) for o in range(1, NZ)
    ]

    for copy in x_copies:
        copy.wait_recv()
    logits = part[0]
    for o in (1, 2, 3):
        logits = logits + decoded(x_in[o - 1], xu_in[o - 1])
    part[0] = logits

    top = jnp.max(logits, axis=0, keepdims=True)
    total = jnp.sum(jnp.exp(logits - top), axis=0, keepdims=True)
    stat[row, 0:1, :] = top
    stat[row, 1:2, :] = total
    base = count[0]
    count[0] += 31

    def stat_copy(o):
        return pltpu.make_async_remote_copy(
            src_ref=stat.at[row], dst_ref=stat.at[row],
            send_sem=send_sem.at[base + o - 1], recv_sem=recv_sem.at[base + o - 1],
            device_id=(d, (row + o) % 32, col), device_id_type=MESH,
        )

    @pl.loop(1, 32)
    def _(o):
        stat_copy(o).start()

    @pl.loop(1, 32)
    def _(o):
        stat_copy(o).wait_recv()

    stats = stat[...]
    tops, totals = stats[:, 0:1, :], stats[:, 1:2, :]
    row_max = jnp.max(tops, axis=0)
    row_sum = jnp.sum(totals * jnp.exp(tops - row_max[None]), axis=0)
    ids = row * V + lax.broadcasted_iota(jnp.int32, (V, C), 0)
    onehot = (tgt[pl.ds(col, 1), :] == ids).astype(F32)
    dlogits = jnp.exp(part[0] - row_max) / row_sum - onehot
    me = d * 8 + col
    dl[me] = dlogits.astype(BF16)

    def spread_x(half, c):
        slot = half * 8 + c
        first = [remote(dl.at[slot], dl.at[slot], x_peer(o)) for o in (1, 2, 3)]
        return first + [remote(dl.at[slot], dl.at[slot], core)]

    def spread_core(half, copies):
        passed = [copies[3]]
        for o in (1, 2, 3):
            copies[o - 1].wait_recv()
            slot = half * 8 + ((x - o) % NX) * 2 + k
            passed.append(remote(dl.at[slot], dl.at[slot], core))
        return passed

    own_x = spread_x(d, col)
    dl_cross = remote(dl.at[me], dl.at[me], dp_peer)
    own_core = spread_core(d, own_x)
    for copy in own_core:
        copy.wait_recv()

    @pl.loop(0, 8)
    def _(c):
        piece = plain_dot(wt[...], dl[d * 8 + c])
        unit = unit_of(piece)
        lanes = pl.ds(pl.multiple_of(c * C, C), C)
        dft[:, lanes] = piece
        y_out[:, lanes] = coded(piece, unit)
        yu_out[:, lanes] = unit

    y_copies = []
    for o in (1, 2, 3):
        quarter = pl.ds(pl.multiple_of(((y + o) % NY) * QD, QD), QD)
        y_copies.append(remote(y_out.at[quarter, :], y_in.at[o - 1], y_peer(o)))
        y_copies.append(remote(yu_out, yu_in.at[o - 1], y_peer(o)))

    hid_cross.wait_recv()
    ho = pl.multiple_of(od * T + col * C, C)
    hid_cols = [
        remote(hid.at[pl.ds(ho, C), :], hid.at[pl.ds(ho, C), :], (d, row, (col + o) % 8))
        for o in range(1, 8)
    ]

    for copy in y_copies:
        copy.wait_recv()
    quarter = dft[pl.ds(pl.multiple_of(y * QD, QD), QD), :]
    for o in (1, 2, 3):
        quarter = quarter + decoded(y_in[o - 1], yu_in[o - 1])
    dft[0:QD, :] = quarter
    unit = unit_of(quarter)
    zu_out[...] = unit
    z_out[...] = coded(quarter, unit)
    z_copies = []
    for o in range(1, NZ):
        block = pl.ds(pl.multiple_of(((z + o) % NZ) * BD, BD), BD)
        z_copies.append(remote(z_out.at[block, :], z_in.at[o - 1], z_peer(o)))
        z_copies.append(remote(zu_out, zu_in.at[o - 1], z_peer(o)))

    for copy in fin_z:
        copy.wait_recv()
    gy = pl.multiple_of(od * T + y * 256, 256)
    fin_y = [
        remote(fin.at[pl.ds(gy, 256), :], fin.at[pl.ds(gy, 256), :], y_peer(o)) for o in (1, 2, 3)
    ]
    dl_cross.wait_recv()
    other_x = spread_x(od, col)

    for copy in z_copies:
        copy.wait_recv()
    block = dft[pl.ds(pl.multiple_of(z * BD, BD), BD), :]
    for o in range(1, NZ):
        block = block + decoded(z_in[o - 1], zu_in[o - 1])
    dfb[y, zz] = block.astype(BF16)

    far = [remote(dfb.at[y, zz], dfb.at[y, zz], ring(o)) for o in (4, 8, -4)]
    other_core = spread_core(od, other_x)
    for copy in hid_cols:
        copy.wait_recv()
    for half in range(2):
        hidt[half] = hid[half * T : half * T + T, :].T
    for copy in far:
        copy.wait_recv()
    near = []
    for o in (1, -1, 2):
        for q in range(4):
            b = (zz + 4 * q) % (2 * NZ)
            near.append(remote(dfb.at[y, b], dfb.at[y, b], ring(o)))
    for copy in near:
        copy.wait_recv()
    along_y = [remote(dfb.at[y], dfb.at[y], y_peer(o)) for o in (1, 2, 3)]

    for copy in fin_y + other_core:
        copy.wait_recv()
    hg[...] = jnp.zeros_like(hg)

    @pl.loop(0, 16)
    def _(c):
        start = pl.multiple_of(c * C, C)
        hg[...] += plain_dot(dl[c], fin[pl.ds(start, C), :])

    for copy in along_y:
        copy.wait_recv()
    dg[...] = tokens_dot(hidt[0], dfb[:, 0:NZ].reshape(D, T)) + tokens_dot(
        hidt[1], dfb[:, NZ : 2 * NZ].reshape(D, T)
    )

    rtile[col] = jnp.zeros((8, 128), F32)
    hsq = hg[...] * hg[...]
    dsq = dg[...] * dg[...]
    mine = rtile.at[col]
    lanes_to_tile(mine, 0, column_to_lanes(jnp.sum(hsq, axis=1, keepdims=True)))
    down_lanes = column_to_lanes(jnp.sum(dsq, axis=1, keepdims=True))
    mine[4:5, :] = down_lanes[:, 0:128]
    mine[5:6, :] = down_lanes[:, 128:256]
    mine[6:7, 0:64] = down_lanes[:, 256:320]
    copies = [remote(rtile.at[col], rtile.at[col], (d, row, (col + o) % 8)) for o in range(1, 8)]
    for copy in copies:
        copy.wait_recv()
    rsum = jnp.sum(rtile[...], axis=0)
    hr = DECAY_RATE * hro[...] + (1.0 - DECAY_RATE) * (
        tile_to_lanes(rsum, 0, 4) * (1.0 / FULL_D) + EPS_SQUARE
    )
    dr = DECAY_RATE * dro[...] + (1.0 - DECAY_RATE) * (
        tile_to_lanes(rsum, 4, 3)[:, 0:FF] * (1.0 / FULL_D) + EPS_SQUARE
    )
    hrows[...] = hr
    drows[...] = dr
    hr_col = lanes_to_column(hr)
    dr_col = lanes_to_column(dr)

    mine = ctile.at[y]
    lanes_to_tile(mine, 0, jnp.sum(hsq, axis=0, keepdims=True))
    lanes_to_tile(mine, 4, jnp.sum(dsq, axis=0, keepdims=True))
    lanes_to_tile(mine, 8, jnp.sum(hsq / hr_col, axis=0, keepdims=True))
    lanes_to_tile(mine, 12, jnp.sum(dsq / dr_col, axis=0, keepdims=True))
    copies = [remote(ctile.at[y], ctile.at[y], y_peer(o)) for o in (1, 2, 3)]
    for copy in copies:
        copy.wait_recv()
    ztile[z] = jnp.sum(ctile[...], axis=0)
    copies = [remote(ztile.at[z], ztile.at[z], z_peer(o)) for o in range(1, NZ)]
    for copy in copies:
        copy.wait_recv()
    csum = jnp.sum(ztile[...], axis=0)
    hc = DECAY_RATE * hco[...] + (1.0 - DECAY_RATE) * (
        tile_to_lanes(csum, 0, 4) * (1.0 / FULL_V) + EPS_SQUARE
    )
    dc = DECAY_RATE * dco[...] + (1.0 - DECAY_RATE) * (
        tile_to_lanes(csum, 4, 4) * (1.0 / FULL_FF) + EPS_SQUARE
    )
    hcols[...] = hc
    dcols[...] = dc
    hs = jnp.sum(tile_to_lanes(csum, 8, 4) / hc, axis=1, keepdims=True)
    ds = jnp.sum(tile_to_lanes(csum, 12, 4) / dc, axis=1, keepdims=True)
    stile[col, 0:1, :] = jnp.broadcast_to(hs, (1, 128))
    stile[col, 1:2, :] = jnp.broadcast_to(ds, (1, 128))
    copies = [remote(stile.at[col], stile.at[col], (d, row, (col + o) % 8)) for o in range(1, 8)]
    hup[...] = hg[...] * lax.rsqrt(hr_col) * lax.rsqrt(hc)
    dup[...] = dg[...] * lax.rsqrt(dr_col) * lax.rsqrt(dc)
    for copy in copies:
        copy.wait_recv()
    squares = jnp.sum(stile[...], axis=0)

    def clip(square_total, entries):
        return 1.0 / jnp.maximum(1.0, jnp.sqrt(square_total * (1.0 / entries)) / CLIP_LEVEL)

    hup[...] = hup[...] * clip(squares[0:1, 0:1], FULL_V * FULL_D)
    dup[...] = dup[...] * clip(squares[1:2, 0:1], FULL_FF * FULL_D)

    for copy in pending:
        copy.wait_send()

    @pl.loop(1, 32)
    def _(o):
        stat_copy(o).wait_send()


N_SEM = 160


def local(fin, w, hid, tgt, hro, hco, dro, dco):
    sds = jax.ShapeDtypeStruct
    vm = pltpu.VMEM
    hbm = pl.BlockSpec(memory_space=pl.ANY)
    vmem = pl.BlockSpec(memory_space=pltpu.VMEM)
    out = pl.pallas_call(
        body,
        out_shape=(
            sds((V, D), F32), sds((1, V), F32), sds((1, D), F32),
            sds((FF, D), F32), sds((1, FF), F32), sds((1, D), F32),
        ),
        in_specs=[hbm] * 3 + [vmem] * 5,
        out_specs=(vmem,) * 6,
        scratch_shapes=[
            vm((2 * T, D), BF16),
            vm((V, D), BF16),
            vm((D, V), BF16),
            vm((2 * T, FF), BF16),
            vm((2, FF, T), BF16),
            vm((16, V, C), BF16),
            vm((4, V, C), F32),
            vm((4, V, C), F32),
            vm((4, V, C), F32),
            vm((3, V, C), I16),
            vm((3, V, C), I16),
            vm((3, 1, C), F32),
            vm((3, 1, C), F32),
            vm((32, 2, C), F32),
            vm((D, T), F32),
            vm((D, T), I16),
            vm((3, QD, T), I16),
            vm((1, T), F32),
            vm((3, 1, T), F32),
            vm((QD, T), I16),
            vm((NZ - 1, BD, T), I16),
            vm((1, T), F32),
            vm((NZ - 1, 1, T), F32),
            vm((NY, 2 * NZ, BD, T), BF16),
            vm((V, D), F32),
            vm((FF, D), F32),
            vm((8, 8, 128), F32),
            vm((NY, 16, 128), F32),
            vm((NZ, 16, 128), F32),
            vm((8, 2, 128), F32),
            pltpu.SemaphoreType.DMA((3,)),
            pltpu.SemaphoreType.DMA((N_SEM,)),
            pltpu.SemaphoreType.DMA((N_SEM,)),
        ],
        compiler_params=pltpu.CompilerParams(
            collective_id=0, has_side_effects=True, vmem_limit_bytes=56 << 20
        ),
    )(
        fin, w, hid, tgt.reshape(8, C), hro.reshape(1, V), hco.reshape(1, D),
        dro.reshape(1, FF), dco.reshape(1, D),
    )
    hup, hrows, hcols, dup, drows, dcols = out
    return (hup, hrows.reshape(V), hcols.reshape(D), dup, drows.reshape(FF), dcols.reshape(D))


def solution(mesh):
    return jax.shard_map(
        local,
        mesh=mesh,
        in_specs=(
            P("dp", "col"),
            P("row", "col"),
            P("dp", "row"),
            P("dp"),
            P("row"),
            P("col"),
            P("row"),
            P("col"),
        ),
        out_specs=(P("row", "col"), P("row"), P("col"), P("row", "col"), P("row"), P("col")),
        check_vma=False,
    )
```

```python
import jax
import jax.numpy as jnp
from jax import lax
from jax.experimental import pallas as pl
from jax.experimental.pallas import tpu as pltpu
from jax.sharding import PartitionSpec as P

EPS_SQUARE = 1e-30
DECAY_RATE = 1.0 - 10.0 ** (-0.8)
CLIP_LEVEL = 1.0
F32, BF16, I16 = jnp.float32, jnp.bfloat16, jnp.int16
MESH = pl.DeviceIdType.MESH

NZ, NY, NX = 8, 4, 4
T = 1024
V = 512
D = 512
FF = 320
C = 128
FULL_V, FULL_D, FULL_FF = 16384, 4096, 10240
QD = D // NY
BD = QD // NZ
LIMIT = 32766.0
PARTS = ((0, 1), (3, 2))


def tokens_dot(left, right):
    return lax.dot_general(left, right, (((1,), (1,)), ((), ())), preferred_element_type=F32)


def plain_dot(left, right):
    return jnp.dot(left, right, preferred_element_type=F32)


def unit_of(values):
    peak = jnp.max(jnp.abs(values), axis=0, keepdims=True)
    return jnp.maximum(peak, 1e-30) * (1.0 / LIMIT)


def coded(values, unit):
    return jnp.round(values * (1.0 / unit)).astype(jnp.int32).astype(I16)


def decoded(codes, unit):
    return codes.astype(jnp.int32).astype(F32) * unit


def lanes_to_tile(ref, row, vector):
    for part in range(vector.shape[1] // 128):
        ref[pl.ds(row + part, 1), :] = vector[:, 128 * part : 128 * part + 128]


def tile_to_lanes(tile, row, parts):
    return jnp.concatenate([tile[row + p : row + p + 1, :] for p in range(parts)], axis=1)


def column_to_lanes(column):
    return jnp.broadcast_to(column, (column.shape[0], 128)).T[0:1, :]


def lanes_to_column(vector):
    return jnp.broadcast_to(vector, (128, vector.shape[1])).T[:, 0:1]


def body(
    fin_in, w_in, hid_in, tgt, hro, hco, dro, dco,
    hup, hrows, hcols, dup, drows, dcols, clips,
    fin, w, wt, hid, dl,
    part, core_out, core_in, x_out, x_in, xu_out, xu_in,
    stat, dft, y_out, y_in, yu_out, yu_in, z_out, z_in, zu_out, zu_in,
    dfb, hg, rtile, ctile, ztile, stile,
    local_sem, send_sem, recv_sem,
):
    d, row, col = lax.axis_index("dp"), lax.axis_index("row"), lax.axis_index("col")
    z, y, x, k = row // NY, row % NY, col // 2, col % 2
    zz = d * NZ + z
    od = 1 - d

    def at(dd, z_, y_, c_):
        return (dd, z_ * NY + y_, c_)

    def ring(o):
        q = (zz + o) % (2 * NZ)
        return at(q // NZ, q % NZ, y, col)

    def x_peer(o):
        return (d, row, ((x + o) % NX) * 2 + k)

    def y_peer(o):
        return at(d, z, (y + o) % NY, col)

    def z_peer(o):
        return at(d, (z + o) % NZ, y, col)

    core = (d, row, 2 * x + 1 - k)
    dp_peer = (od, row, col)

    pending = []
    count = [0]

    def remote(src, dst, device, slot=None):
        if slot is None:
            slot = count[0]
            count[0] += 1
        copy = pltpu.make_async_remote_copy(
            src_ref=src, dst_ref=dst, send_sem=send_sem.at[slot], recv_sem=recv_sem.at[slot],
            device_id=device, device_id_type=MESH,
        )
        copy.start()
        pending.append(copy)
        return copy

    loads = [
        pltpu.make_async_copy(fin_in, fin.at[pl.ds(d * T, T), :], local_sem.at[0]),
        pltpu.make_async_copy(w_in, w, local_sem.at[1]),
        pltpu.make_async_copy(hid_in, hid.at[d], local_sem.at[2]),
    ]
    for load in loads:
        load.start()

    barrier = pltpu.get_barrier_semaphore()

    def greet(device):
        pl.semaphore_signal(barrier, inc=1, device_id=device, device_id_type=MESH)

    @pl.loop(1, 32)
    def _(o):
        greet((d, (row + o) % 32, col))

    @pl.loop(1, 8)
    def _(o):
        greet((d, row, (col + o) % 8))

    @pl.loop(0, NZ)
    def _(o):
        greet(at(od, o, y, col))

    for load in loads:
        load.wait()

    def logits_part(c):
        start = pl.multiple_of(d * T + c * C, C)
        return tokens_dot(w[...], fin[pl.ds(start, C), :])

    for o in (1, 2, 3, 0):
        xo = (x + o) % NX
        core_out[o] = logits_part(2 * xo + 1 - k)
        part[o] = logits_part(2 * xo + k)
    wt[...] = w[...].T
    pl.semaphore_wait(barrier, 31 + 7 + NZ)

    core_copies = {}
    for o in (1, 2, 3, 0):
        core_copies[o] = remote(core_out.at[o], core_in.at[o], core)
    fq = pl.multiple_of(d * T + (y * NZ + z) * 32, 32)
    fin_cross = [
        remote(fin.at[pl.ds(fq, 32), :], fin.at[pl.ds(fq, 32), :], at(od, (z + o) % NZ, y, col))
        for o in range(NZ)
    ]
    x_copies = []
    for o in (1, 2, 3):
        core_copies[o].wait_recv()
        total = part[o] + core_in[o]
        unit = unit_of(total)
        x_out[o - 1] = coded(total, unit)
        xu_out[o - 1] = unit
        x_copies.append(remote(x_out.at[o - 1], x_in.at[o - 1], x_peer(o)))
        x_copies.append(remote(xu_out.at[o - 1], xu_in.at[o - 1], x_peer(o)))
    core_copies[0].wait_recv()
    part[0] = part[0] + core_in[0]

    for copy in x_copies:
        copy.wait_recv()
    logits = part[0]
    for o in (1, 2, 3):
        logits = logits + decoded(x_in[o - 1], xu_in[o - 1])
    part[0] = logits

    top = jnp.max(logits, axis=0, keepdims=True)
    total = jnp.sum(jnp.exp(logits - top), axis=0, keepdims=True)
    stat[row, 0:1, :] = top
    stat[row, 1:2, :] = total
    base = count[0]
    count[0] += 31

    def stat_copy(o):
        return pltpu.make_async_remote_copy(
            src_ref=stat.at[row], dst_ref=stat.at[row],
            send_sem=send_sem.at[base + o - 1], recv_sem=recv_sem.at[base + o - 1],
            device_id=(d, (row + o) % 32, col), device_id_type=MESH,
        )

    @pl.loop(1, 32)
    def _(o):
        stat_copy(o).start()

    @pl.loop(1, 32)
    def _(o):
        stat_copy(o).wait_recv()

    stats = stat[...]
    tops, totals = stats[:, 0:1, :], stats[:, 1:2, :]
    row_max = jnp.max(tops, axis=0)
    row_sum = jnp.sum(totals * jnp.exp(tops - row_max[None]), axis=0)
    ids = row * V + lax.broadcasted_iota(jnp.int32, (V, C), 0)
    onehot = (tgt[pl.ds(col, 1), :] == ids).astype(F32)
    dlogits = jnp.exp(part[0] - row_max) / row_sum - onehot
    me = d * 8 + col
    dl[me] = dlogits.astype(BF16)

    def spread_x(half, c):
        slot = half * 8 + c
        first = [remote(dl.at[slot], dl.at[slot], x_peer(o)) for o in (1, 2, 3)]
        return first + [remote(dl.at[slot], dl.at[slot], core)]

    def pass_core(half, copies, o):
        copies[o - 1].wait_recv()
        slot = half * 8 + ((x - o) % NX) * 2 + k
        return remote(dl.at[slot], dl.at[slot], core)

    own_x = spread_x(d, col)
    dl_cross = remote(dl.at[me], dl.at[me], dp_peer)
    hq = pl.ds(pl.multiple_of(col * C, C), C)
    hid_cross = remote(hid.at[d, :, hq], hid.at[d, :, hq], dp_peer)
    own_core = {0: own_x[3]}
    own_core[1] = pass_core(d, own_x, 1)
    for copy in fin_cross:
        copy.wait_recv()
    gy = pl.multiple_of(od * T + y * 256, 256)
    fin_y = [
        remote(fin.at[pl.ds(gy, 256), :], fin.at[pl.ds(gy, 256), :], y_peer(o)) for o in (1, 2, 3)
    ]
    own_core[3] = pass_core(d, own_x, 3)
    own_core[2] = pass_core(d, own_x, 2)

    y_copies = []
    for p, offsets in enumerate(PARTS):
        for j, o in enumerate(offsets):
            own_core[o].wait_recv()
            for core_ in range(2):
                piece = plain_dot(wt[...], dl[d * 8 + ((x - o) % NX) * 2 + core_])
                unit = unit_of(piece)
                lanes = slice((2 * j + core_) * C, (2 * j + core_ + 1) * C)
                dft[p, :, lanes] = piece
                y_out[p, :, lanes] = coded(piece, unit)
                yu_out[p, :, lanes] = unit
        copies = []
        for o in (1, 2, 3):
            quarter = pl.ds(pl.multiple_of(((y + o) % NY) * QD, QD), QD)
            copies.append(remote(y_out.at[p, quarter, :], y_in.at[p, o - 1], y_peer(o)))
            copies.append(remote(yu_out.at[p], yu_in.at[p, o - 1], y_peer(o)))
        y_copies.append(copies)

    def head_part(half):
        total = None
        for pair in range(4):
            both = jnp.concatenate([dl[half * 8 + 2 * pair], dl[half * 8 + 2 * pair + 1]], axis=1)
            start = pl.multiple_of(half * T + pair * 2 * C, 2 * C)
            product = plain_dot(both, fin[pl.ds(start, 2 * C), :])
            total = product if total is None else total + product
        return total

    hg[d] = head_part(d)

    dl_cross.wait_recv()
    other_x = spread_x(od, col)

    z_copies = []
    for p in range(2):
        for copy in y_copies[p]:
            copy.wait_recv()
        quarter = dft[p, pl.ds(pl.multiple_of(y * QD, QD), QD), :]
        for o in (1, 2, 3):
            quarter = quarter + decoded(y_in[p, o - 1], yu_in[p, o - 1])
        dft[p, 0:QD, :] = quarter
        unit = unit_of(quarter)
        zu_out[p] = unit
        z_out[p] = coded(quarter, unit)
        copies = []
        for o in range(1, NZ):
            block = pl.ds(pl.multiple_of(((z + o) % NZ) * BD, BD), BD)
            copies.append(remote(z_out.at[p, block, :], z_in.at[p, o - 1], z_peer(o)))
            copies.append(remote(zu_out.at[p], zu_in.at[p, o - 1], z_peer(o)))
        z_copies.append(copies)

    hid_cross.wait_recv()
    hid_cols = [
        remote(hid.at[od, :, hq], hid.at[od, :, hq], (d, row, (col + o) % 8)) for o in range(1, 8)
    ]
    other_core = [other_x[3]] + [pass_core(od, other_x, o) for o in (1, 3, 2)]

    for p in range(2):
        for copy in z_copies[p]:
            copy.wait_recv()
        block = dft[p, pl.ds(pl.multiple_of(z * BD, BD), BD), :]
        for o in range(1, NZ):
            block = block + decoded(z_in[p, o - 1], zu_in[p, o - 1])
        dfb[y, zz, :, p * 512 : p * 512 + 512] = block.astype(BF16)

    def block_to(b, device):
        return remote(dfb.at[y, b], dfb.at[y, b], device)

    along_y = []

    def share_y(b):
        for o in (1, 2, 3):
            along_y.append(block_to(b, y_peer(o)))

    far = {o: block_to(zz, ring(o)) for o in (8, 4, -4)}
    near = {(o, 0): block_to(zz, ring(o)) for o in (1, -1, 2)}
    share_y(zz)
    for copy in fin_y + other_core:
        copy.wait_recv()
    hg[od] = head_part(od)
    for o in (1, -1, 2):
        near[o, 0].wait_recv()
        share_y((zz - o) % (2 * NZ))
    for q in (4, -4, 8):
        far[q].wait_recv()
        b = (zz - q) % (2 * NZ)
        for o in (1, -1, 2):
            near[o, q] = block_to(b, ring(o))
        share_y(b)
    hg[0] = hg[0] + hg[1]
    for q in (4, -4, 8):
        for o in (1, -1, 2):
            near[o, q].wait_recv()
            share_y((zz - o - q) % (2 * NZ))
    for copy in hid_cols:
        copy.wait_recv()
    for copy in along_y:
        copy.wait_recv()
    down = None
    for half in range(2):
        for p, offsets in enumerate(PARTS):
            for j, o in enumerate(offsets):
                tokens = pl.ds(pl.multiple_of(((x - o) % NX) * 2 * C, 2 * C), 2 * C)
                first = p * 512 + j * 256
                right = dfb[:, half * NZ : half * NZ + NZ, :, first : first + 256].reshape(D, 2 * C)
                product = tokens_dot(hid[half, :, tokens], right)
                down = product if down is None else down + product

    rtile[col] = jnp.zeros((8, 128), F32)
    hsq = hg[0] * hg[0]
    dsq = down * down
    mine = rtile.at[col]
    lanes_to_tile(mine, 0, column_to_lanes(jnp.sum(hsq, axis=1, keepdims=True)))
    down_lanes = column_to_lanes(jnp.sum(dsq, axis=1, keepdims=True))
    mine[4:5, :] = down_lanes[:, 0:128]
    mine[5:6, :] = down_lanes[:, 128:256]
    mine[6:7, 0:64] = down_lanes[:, 256:320]
    copies = [remote(rtile.at[col], rtile.at[col], (d, row, (col + o) % 8)) for o in range(1, 8)]
    for copy in copies:
        copy.wait_recv()
    rsum = jnp.sum(rtile[...], axis=0)
    hr = DECAY_RATE * hro[...].reshape(1, V) + (1.0 - DECAY_RATE) * (
        tile_to_lanes(rsum, 0, 4) * (1.0 / FULL_D) + EPS_SQUARE
    )
    dr = DECAY_RATE * dro[...].reshape(1, FF) + (1.0 - DECAY_RATE) * (
        tile_to_lanes(rsum, 4, 3)[:, 0:FF] * (1.0 / FULL_D) + EPS_SQUARE
    )
    hrows[...] = hr
    drows[...] = dr
    hr_col = lanes_to_column(hr)
    dr_col = lanes_to_column(dr)

    mine = ctile.at[y]
    lanes_to_tile(mine, 0, jnp.sum(hsq, axis=0, keepdims=True))
    lanes_to_tile(mine, 4, jnp.sum(dsq, axis=0, keepdims=True))
    lanes_to_tile(mine, 8, jnp.sum(hsq / hr_col, axis=0, keepdims=True))
    lanes_to_tile(mine, 12, jnp.sum(dsq / dr_col, axis=0, keepdims=True))
    copies = [remote(ctile.at[y], ctile.at[y], y_peer(o)) for o in (1, 2, 3)]
    for copy in copies:
        copy.wait_recv()
    ztile[z] = jnp.sum(ctile[...], axis=0)
    copies = [remote(ztile.at[z], ztile.at[z], z_peer(o)) for o in range(1, NZ)]
    for copy in copies:
        copy.wait_recv()
    csum = jnp.sum(ztile[...], axis=0)
    hc = DECAY_RATE * hco[...].reshape(1, D) + (1.0 - DECAY_RATE) * (
        tile_to_lanes(csum, 0, 4) * (1.0 / FULL_V) + EPS_SQUARE
    )
    dc = DECAY_RATE * dco[...].reshape(1, D) + (1.0 - DECAY_RATE) * (
        tile_to_lanes(csum, 4, 4) * (1.0 / FULL_FF) + EPS_SQUARE
    )
    hcols[...] = hc
    dcols[...] = dc
    hs = jnp.sum(tile_to_lanes(csum, 8, 4) / hc, axis=1, keepdims=True)
    ds = jnp.sum(tile_to_lanes(csum, 12, 4) / dc, axis=1, keepdims=True)
    stile[col, 0:1, :] = jnp.broadcast_to(hs, (1, 128))
    stile[col, 1:2, :] = jnp.broadcast_to(ds, (1, 128))
    copies = [remote(stile.at[col], stile.at[col], (d, row, (col + o) % 8)) for o in range(1, 8)]
    hup[...] = hg[0] * lax.rsqrt(hr_col) * lax.rsqrt(hc)
    dup[...] = down * lax.rsqrt(dr_col) * lax.rsqrt(dc)
    for copy in copies:
        copy.wait_recv()
    clips[...] = jnp.sum(stile[...], axis=0)

    for copy in pending:
        copy.wait_send()

    @pl.loop(1, 32)
    def _(o):
        stat_copy(o).wait_send()


def finish(hraw, hr, hc, draw, dr, dc, squares, hup, hrows, hcols, dup, drows, dcols):
    def clip(square_total, entries):
        return 1.0 / jnp.maximum(1.0, jnp.sqrt(square_total * (1.0 / entries)) / CLIP_LEVEL)

    hup[...] = hraw[...] * clip(squares[0:1, 0:1], FULL_V * FULL_D)
    dup[...] = draw[...] * clip(squares[1:2, 0:1], FULL_FF * FULL_D)
    hrows[...] = hr[...].reshape(V)
    hcols[...] = hc[...].reshape(D)
    drows[...] = dr[...].reshape(FF)
    dcols[...] = dc[...].reshape(D)


N_SEM = 256


def local(fin, w, hid, tgt, hro, hco, dro, dco):
    sds = jax.ShapeDtypeStruct
    vm = pltpu.VMEM
    hbm = pl.BlockSpec(memory_space=pl.ANY)
    vmem = pl.BlockSpec(memory_space=pltpu.VMEM)
    raw = pl.pallas_call(
        body,
        out_shape=(
            sds((V, D), F32), sds((1, V), F32), sds((1, D), F32),
            sds((FF, D), F32), sds((1, FF), F32), sds((1, D), F32), sds((2, 128), F32),
        ),
        in_specs=[hbm] * 3 + [vmem] * 5,
        out_specs=(vmem,) * 7,
        scratch_shapes=[
            vm((2 * T, D), BF16),
            vm((V, D), BF16),
            vm((D, V), BF16),
            vm((2, FF, T), BF16),
            vm((16, V, C), BF16),
            vm((4, V, C), F32),
            vm((4, V, C), F32),
            vm((4, V, C), F32),
            vm((3, V, C), I16),
            vm((3, V, C), I16),
            vm((3, 1, C), F32),
            vm((3, 1, C), F32),
            vm((32, 2, C), F32),
            vm((2, D, T // 2), F32),
            vm((2, D, T // 2), I16),
            vm((2, 3, QD, T // 2), I16),
            vm((2, 1, T // 2), F32),
            vm((2, 3, 1, T // 2), F32),
            vm((2, QD, T // 2), I16),
            vm((2, NZ - 1, BD, T // 2), I16),
            vm((2, 1, T // 2), F32),
            vm((2, NZ - 1, 1, T // 2), F32),
            vm((NY, 2 * NZ, BD, T), BF16),
            vm((2, V, D), F32),
            vm((8, 8, 128), F32),
            vm((NY, 16, 128), F32),
            vm((NZ, 16, 128), F32),
            vm((8, 2, 128), F32),
            pltpu.SemaphoreType.DMA((3,)),
            pltpu.SemaphoreType.DMA((N_SEM,)),
            pltpu.SemaphoreType.DMA((N_SEM,)),
        ],
        compiler_params=pltpu.CompilerParams(
            collective_id=0, has_side_effects=True, vmem_limit_bytes=56 << 20
        ),
    )(fin, w, hid.T, tgt.reshape(8, C), hro, hco, dro, dco)
    return pl.pallas_call(
        finish,
        out_shape=(
            sds((V, D), F32), sds((V,), F32), sds((D,), F32),
            sds((FF, D), F32), sds((FF,), F32), sds((D,), F32),
        ),
        in_specs=[vmem] * 7,
        out_specs=(vmem,) * 6,
        compiler_params=pltpu.CompilerParams(vmem_limit_bytes=16 << 20),
    )(*raw)


def solution(mesh):
    return jax.shard_map(
        local,
        mesh=mesh,
        in_specs=(
            P("dp", "col"),
            P("row", "col"),
            P("dp", "row"),
            P("dp"),
            P("row"),
            P("col"),
            P("row"),
            P("col"),
        ),
        out_specs=(P("row", "col"), P("row"), P("col"), P("row", "col"), P("row"), P("col")),
        check_vma=False,
    )
```

```python
import jax
import jax.numpy as jnp
from jax import lax
from jax.experimental import pallas as pl
from jax.experimental.pallas import tpu as pltpu
from jax.sharding import PartitionSpec as P

EPS_SQUARE = 1e-30
DECAY_RATE = 1.0 - 10.0 ** (-0.8)
CLIP_LEVEL = 1.0
F32, BF16, I16 = jnp.float32, jnp.bfloat16, jnp.int16
MESH = pl.DeviceIdType.MESH

NZ, NY, NX = 8, 4, 4
T = 1024
V = 512
D = 512
FF = 320
C = 128
FULL_V, FULL_D, FULL_FF = 16384, 4096, 10240
QD = D // NY
BD = QD // NZ
LIMIT = 32766.0
PARTS = ((0, 1), (3, 2))


def tokens_dot(left, right):
    return lax.dot_general(left, right, (((1,), (1,)), ((), ())), preferred_element_type=F32)


def plain_dot(left, right):
    return jnp.dot(left, right, preferred_element_type=F32)


def unit_of(values):
    peak = jnp.max(jnp.abs(values), axis=0, keepdims=True)
    return jnp.maximum(peak, 1e-30) * (1.0 / LIMIT)


def coded(values, unit):
    return jnp.round(values * (1.0 / unit)).astype(jnp.int32).astype(I16)


def decoded(codes, unit):
    return codes.astype(jnp.int32).astype(F32) * unit


def lanes_to_tile(ref, row, vector):
    for part in range(vector.shape[1] // 128):
        ref[pl.ds(row + part, 1), :] = vector[:, 128 * part : 128 * part + 128]


def tile_to_lanes(tile, row, parts):
    return jnp.concatenate([tile[row + p : row + p + 1, :] for p in range(parts)], axis=1)


def column_to_lanes(column):
    return jnp.broadcast_to(column, (column.shape[0], 128)).T[0:1, :]


def lanes_to_column(vector):
    return jnp.broadcast_to(vector, (128, vector.shape[1])).T[:, 0:1]


def body(
    fin_in, w_in, hid_in, tgt, hro, hco, dro, dco,
    hup, hrows, hcols, dup, drows, dcols, clips,
    fin, w, wt, hid, dl,
    both, core_in, x_out, x_in, xu_out, xu_in,
    stat, dft, y_out, y_in, yu_out, yu_in, z_out, z_in, zu_out, zu_in,
    dfb, hg, dq, d_out, d_in, du_out, du_in, rtile, ctile, ztile, stile,
    local_sem, send_sem, recv_sem,
):
    d, row, col = lax.axis_index("dp"), lax.axis_index("row"), lax.axis_index("col")
    z, y, x, k = row // NY, row % NY, col // 2, col % 2
    zz = d * NZ + z
    od = 1 - d

    def at(dd, z_, y_, c_):
        return (dd, z_ * NY + y_, c_)

    def ring(o):
        q = (zz + o) % (2 * NZ)
        return at(q // NZ, q % NZ, y, col)

    def x_peer(o):
        return (d, row, ((x + o) % NX) * 2 + k)

    def y_peer(o):
        return at(d, z, (y + o) % NY, col)

    def z_peer(o):
        return at(d, (z + o) % NZ, y, col)

    core = (d, row, 2 * x + 1 - k)
    dp_peer = (od, row, col)
    mirror = at(od, NZ - 1 - z, y, col)

    pending = []
    count = [0]

    def remote(src, dst, device, slot=None):
        if slot is None:
            slot = count[0]
            count[0] += 1
        copy = pltpu.make_async_remote_copy(
            src_ref=src, dst_ref=dst, send_sem=send_sem.at[slot], recv_sem=recv_sem.at[slot],
            device_id=device, device_id_type=MESH,
        )
        copy.start()
        pending.append(copy)
        return copy

    loads = [
        pltpu.make_async_copy(fin_in, fin.at[pl.ds(d * T, T), :], local_sem.at[0]),
        pltpu.make_async_copy(w_in, w, local_sem.at[1]),
        pltpu.make_async_copy(hid_in, hid.at[d, y], local_sem.at[2]),
    ]
    for load in loads:
        load.start()

    barrier = pltpu.get_barrier_semaphore()

    def greet(device):
        pl.semaphore_signal(barrier, inc=1, device_id=device, device_id_type=MESH)

    @pl.loop(1, 32)
    def _(o):
        greet((d, (row + o) % 32, col))

    @pl.loop(1, 8)
    def _(o):
        greet((d, row, (col + o) % 8))

    others = [dp_peer, mirror] + [ring(o) for o in (1, -1, 2, -2, 4, -4)]
    for device in others:
        greet(device)

    for load in loads:
        load.wait()

    for o in (1, 2, 3, 0):
        start = pl.multiple_of(d * T + ((x + o) % NX) * 2 * C, 2 * C)
        pair = tokens_dot(w[...], fin[pl.ds(start, 2 * C), :])
        both[0, o] = pair[:, 0:C]
        both[1, o] = pair[:, C : 2 * C]
    part = both.at[k]
    wt[...] = w[...].T
    pl.semaphore_wait(barrier, 31 + 7 + len(others))

    core_copies = {}
    for o in (1, 2, 3, 0):
        core_copies[o] = remote(both.at[1 - k, o], core_in.at[o], core)
    fq = pl.ds(pl.multiple_of(d * T + (y * NZ + z) * 32, 32), 32)
    gq = pl.ds(pl.multiple_of(od * T + (y * NZ + NZ - 1 - z) * 32, 32), 32)
    fin_cross = remote(fin.at[fq, :], fin.at[fq, :], mirror)
    hq = pl.ds(pl.multiple_of(col * C, C), C)
    hid_cross = remote(hid.at[d, y, :, hq], hid.at[d, y, :, hq], dp_peer)
    hid_y = [remote(hid.at[d, y], hid.at[d, y], y_peer(o)) for o in (1, 2, 3)]
    x_copies = []
    for o in (1, 2, 3):
        core_copies[o].wait_recv()
        total = part[o] + core_in[o]
        unit = unit_of(total)
        x_out[o - 1] = coded(total, unit)
        xu_out[o - 1] = unit
        x_copies.append(remote(x_out.at[o - 1], x_in.at[o - 1], x_peer(o)))
        x_copies.append(remote(xu_out.at[o - 1], xu_in.at[o - 1], x_peer(o)))
    core_copies[0].wait_recv()
    part[0] = part[0] + core_in[0]
    fin_cross.wait_recv()
    fin_z = [remote(fin.at[gq, :], fin.at[gq, :], z_peer(o)) for o in range(1, NZ)]

    for copy in x_copies:
        copy.wait_recv()
    logits = part[0]
    for o in (1, 2, 3):
        logits = logits + decoded(x_in[o - 1], xu_in[o - 1])
    part[0] = logits

    top = jnp.max(logits, axis=0, keepdims=True)
    total = jnp.sum(jnp.exp(logits - top), axis=0, keepdims=True)
    stat[row, 0:1, :] = top
    stat[row, 1:2, :] = total
    base = count[0]
    count[0] += 31

    def stat_copy(o):
        return pltpu.make_async_remote_copy(
            src_ref=stat.at[row], dst_ref=stat.at[row],
            send_sem=send_sem.at[base + o - 1], recv_sem=recv_sem.at[base + o - 1],
            device_id=(d, (row + o) % 32, col), device_id_type=MESH,
        )

    @pl.loop(1, 32)
    def _(o):
        stat_copy(o).start()

    @pl.loop(1, 32)
    def _(o):
        stat_copy(o).wait_recv()

    stats = stat[...]
    tops, totals = stats[:, 0:1, :], stats[:, 1:2, :]
    row_max = jnp.max(tops, axis=0)
    row_sum = jnp.sum(totals * jnp.exp(tops - row_max[None]), axis=0)
    ids = row * V + lax.broadcasted_iota(jnp.int32, (V, C), 0)
    onehot = (tgt[pl.ds(col, 1), :] == ids).astype(F32)
    dlogits = jnp.exp(part[0] - row_max) / row_sum - onehot
    me = d * 8 + col
    dl[me] = dlogits.astype(BF16)

    def spread_x(half, c):
        slot = half * 8 + c
        first = [remote(dl.at[slot], dl.at[slot], x_peer(o)) for o in (1, 2, 3)]
        return first + [remote(dl.at[slot], dl.at[slot], core)]

    def pass_core(half, copies, o):
        copies[o - 1].wait_recv()
        slot = half * 8 + ((x - o) % NX) * 2 + k
        return remote(dl.at[slot], dl.at[slot], core)

    own_x = spread_x(d, col)
    dl_cross = remote(dl.at[me], dl.at[me], dp_peer)
    own_core = {0: own_x[3]}
    own_core[1] = pass_core(d, own_x, 1)
    own_core[3] = pass_core(d, own_x, 3)
    hid_cross.wait_recv()
    hid_y += [remote(hid.at[od, y, :, hq], hid.at[od, y, :, hq], y_peer(o)) for o in (1, 2, 3)]
    own_core[2] = pass_core(d, own_x, 2)

    y_copies = []
    for p, offsets in enumerate(PARTS):
        for j, o in enumerate(offsets):
            own_core[o].wait_recv()
            for core_ in range(2):
                piece = plain_dot(wt[...], dl[d * 8 + ((x - o) % NX) * 2 + core_])
                unit = unit_of(piece)
                lanes = slice((2 * j + core_) * C, (2 * j + core_ + 1) * C)
                dft[p, :, lanes] = piece
                y_out[p, :, lanes] = coded(piece, unit)
                yu_out[p, :, lanes] = unit
        copies = []
        for o in (1, 2, 3):
            quarter = pl.ds(pl.multiple_of(((y + o) % NY) * QD, QD), QD)
            copies.append(remote(y_out.at[p, quarter, :], y_in.at[p, o - 1], y_peer(o)))
            copies.append(remote(yu_out.at[p], yu_in.at[p, o - 1], y_peer(o)))
        y_copies.append(copies)

    for copy in hid_y:
        copy.wait_recv()
    hid_x = [remote(hid.at[od, :, :, hq], hid.at[od, :, :, hq], x_peer(o)) for o in (1, 2, 3)]
    hid_core = [remote(hid.at[od, :, :, hq], hid.at[od, :, :, hq], core)]

    def head_part(half):
        total = None
        for pair in range(4):
            both = jnp.concatenate([dl[half * 8 + 2 * pair], dl[half * 8 + 2 * pair + 1]], axis=1)
            start = pl.multiple_of(half * T + pair * 2 * C, 2 * C)
            product = plain_dot(both, fin[pl.ds(start, 2 * C), :])
            total = product if total is None else total + product
        return total

    hg[d] = head_part(d)

    z_copies = []
    for p in range(2):
        for copy in y_copies[p]:
            copy.wait_recv()
        quarter = dft[p, pl.ds(pl.multiple_of(y * QD, QD), QD), :]
        for o in (1, 2, 3):
            quarter = quarter + decoded(y_in[p, o - 1], yu_in[p, o - 1])
        dft[p, 0:QD, :] = quarter
        unit = unit_of(quarter)
        zu_out[p] = unit
        z_out[p] = coded(quarter, unit)
        copies = []
        for o in range(1, NZ):
            block = pl.ds(pl.multiple_of(((z + o) % NZ) * BD, BD), BD)
            copies.append(remote(z_out.at[p, block, :], z_in.at[p, o - 1], z_peer(o)))
            copies.append(remote(zu_out.at[p], zu_in.at[p, o - 1], z_peer(o)))
        z_copies.append(copies)

    for copy in fin_z:
        copy.wait_recv()
    gy = pl.ds(pl.multiple_of(od * T + y * 256, 256), 256)
    fin_y = [remote(fin.at[gy, :], fin.at[gy, :], y_peer(o)) for o in (1, 2, 3)]
    dl_cross.wait_recv()
    other_x = spread_x(od, col)

    for p in range(2):
        for copy in z_copies[p]:
            copy.wait_recv()
        block = dft[p, pl.ds(pl.multiple_of(z * BD, BD), BD), :]
        for o in range(1, NZ):
            block = block + decoded(z_in[p, o - 1], zu_in[p, o - 1])
        dfb[zz, :, p * 512 : p * 512 + 512] = block.astype(BF16)

    def block_to(b, device):
        return remote(dfb.at[b], dfb.at[b], device)

    near = {}

    def pass_on(q):
        b = (zz - q) % (2 * NZ)
        for o in (1, -1, 2):
            near[o, q] = block_to(b, ring(o))

    far = {o: block_to(zz, ring(o)) for o in (8, 4, -4)}
    pass_on(0)
    other_core = [other_x[3]] + [pass_core(od, other_x, o) for o in (1, 3, 2)]
    for q in (4, -4, 8):
        far[q].wait_recv()
        pass_on(q)
    for o in (1, 3, 2):
        hid_x[o - 1].wait_recv()
        lanes = pl.ds(pl.multiple_of((((x - o) % NX) * 2 + k) * C, C), C)
        hid_core.append(remote(hid.at[od, :, :, lanes], hid.at[od, :, :, lanes], core))
    for copy in fin_y + other_core:
        copy.wait_recv()
    hg[od] = head_part(od)
    hg[0] = hg[0] + hg[1]
    for copy in near.values():
        copy.wait_recv()
    for copy in hid_core:
        copy.wait_recv()
    total = None
    for half in range(2):
        for p, offsets in enumerate(PARTS):
            for j, o in enumerate(offsets):
                tokens = pl.ds(pl.multiple_of(((x - o) % NX) * 2 * C, 2 * C), 2 * C)
                first = p * 512 + j * 256
                right = dfb[half * NZ : half * NZ + NZ, :, first : first + 256].reshape(QD, 2 * C)
                product = tokens_dot(hid[half, :, :, tokens].reshape(NY * FF, 2 * C), right)
                total = product if total is None else total + product
    dq[...] = total.reshape(NY, FF, QD)
    unit = unit_of(total)
    du_out[...] = unit
    d_out[...] = coded(total, unit).reshape(NY, FF, QD)
    swaps = []
    for o in (1, 2, 3):
        swaps.append(remote(d_out.at[(y + o) % NY], d_in.at[y], y_peer(o)))
        swaps.append(remote(du_out, du_in.at[y], y_peer(o)))
    mine = dq[y]
    d_in[y] = d_out[y]
    du_in[y] = unit
    for copy in swaps:
        copy.wait_recv()
    for q in range(NY):
        dq[q] = decoded(d_in[q], du_in[q])
    dq[y] = mine
    down = jnp.concatenate([dq[q] for q in range(NY)], axis=1)

    rtile[col] = jnp.zeros((8, 128), F32)
    hsq = hg[0] * hg[0]
    dsq = down * down
    mine = rtile.at[col]
    lanes_to_tile(mine, 0, column_to_lanes(jnp.sum(hsq, axis=1, keepdims=True)))
    down_lanes = column_to_lanes(jnp.sum(dsq, axis=1, keepdims=True))
    mine[4:5, :] = down_lanes[:, 0:128]
    mine[5:6, :] = down_lanes[:, 128:256]
    mine[6:7, 0:64] = down_lanes[:, 256:320]
    copies = [remote(rtile.at[col], rtile.at[col], (d, row, (col + o) % 8)) for o in range(1, 8)]
    for copy in copies:
        copy.wait_recv()
    rsum = jnp.sum(rtile[...], axis=0)
    hr = DECAY_RATE * hro[...].reshape(1, V) + (1.0 - DECAY_RATE) * (
        tile_to_lanes(rsum, 0, 4) * (1.0 / FULL_D) + EPS_SQUARE
    )
    dr = DECAY_RATE * dro[...].reshape(1, FF) + (1.0 - DECAY_RATE) * (
        tile_to_lanes(rsum, 4, 3)[:, 0:FF] * (1.0 / FULL_D) + EPS_SQUARE
    )
    hrows[...] = hr
    drows[...] = dr
    hr_col = lanes_to_column(hr)
    dr_col = lanes_to_column(dr)

    mine = ctile.at[y]
    lanes_to_tile(mine, 0, jnp.sum(hsq, axis=0, keepdims=True))
    lanes_to_tile(mine, 4, jnp.sum(dsq, axis=0, keepdims=True))
    lanes_to_tile(mine, 8, jnp.sum(hsq / hr_col, axis=0, keepdims=True))
    lanes_to_tile(mine, 12, jnp.sum(dsq / dr_col, axis=0, keepdims=True))
    copies = [remote(ctile.at[y], ctile.at[y], y_peer(o)) for o in (1, 2, 3)]
    for copy in copies:
        copy.wait_recv()
    ztile[z] = jnp.sum(ctile[...], axis=0)
    copies = [remote(ztile.at[z], ztile.at[z], z_peer(o)) for o in range(1, NZ)]
    for copy in copies:
        copy.wait_recv()
    csum = jnp.sum(ztile[...], axis=0)
    hc = DECAY_RATE * hco[...].reshape(1, D) + (1.0 - DECAY_RATE) * (
        tile_to_lanes(csum, 0, 4) * (1.0 / FULL_V) + EPS_SQUARE
    )
    dc = DECAY_RATE * dco[...].reshape(1, D) + (1.0 - DECAY_RATE) * (
        tile_to_lanes(csum, 4, 4) * (1.0 / FULL_FF) + EPS_SQUARE
    )
    hcols[...] = hc
    dcols[...] = dc
    hs = jnp.sum(tile_to_lanes(csum, 8, 4) / hc, axis=1, keepdims=True)
    ds = jnp.sum(tile_to_lanes(csum, 12, 4) / dc, axis=1, keepdims=True)
    stile[col, 0:1, :] = jnp.broadcast_to(hs, (1, 128))
    stile[col, 1:2, :] = jnp.broadcast_to(ds, (1, 128))
    copies = [remote(stile.at[col], stile.at[col], (d, row, (col + o) % 8)) for o in range(1, 8)]
    hup[...] = hg[0] * lax.rsqrt(hr_col) * lax.rsqrt(hc)
    dup[...] = down * lax.rsqrt(dr_col) * lax.rsqrt(dc)
    for copy in copies:
        copy.wait_recv()
    clips[...] = jnp.sum(stile[...], axis=0)

    for copy in pending:
        copy.wait_send()

    @pl.loop(1, 32)
    def _(o):
        stat_copy(o).wait_send()


def finish(hraw, hr, hc, draw, dr, dc, squares, hup, hrows, hcols, dup, drows, dcols):
    def clip(square_total, entries):
        return 1.0 / jnp.maximum(1.0, jnp.sqrt(square_total * (1.0 / entries)) / CLIP_LEVEL)

    hup[...] = hraw[...] * clip(squares[0:1, 0:1], FULL_V * FULL_D)
    dup[...] = draw[...] * clip(squares[1:2, 0:1], FULL_FF * FULL_D)
    hrows[...] = hr[...].reshape(V)
    hcols[...] = hc[...].reshape(D)
    drows[...] = dr[...].reshape(FF)
    dcols[...] = dc[...].reshape(D)


N_SEM = 256


def local(fin, w, hid, tgt, hro, hco, dro, dco):
    sds = jax.ShapeDtypeStruct
    vm = pltpu.VMEM
    hbm = pl.BlockSpec(memory_space=pl.ANY)
    vmem = pl.BlockSpec(memory_space=pltpu.VMEM)
    raw = pl.pallas_call(
        body,
        out_shape=(
            sds((V, D), F32), sds((1, V), F32), sds((1, D), F32),
            sds((FF, D), F32), sds((1, FF), F32), sds((1, D), F32), sds((2, 128), F32),
        ),
        in_specs=[hbm] * 3 + [vmem] * 5,
        out_specs=(vmem,) * 7,
        scratch_shapes=[
            vm((2 * T, D), BF16),
            vm((V, D), BF16),
            vm((D, V), BF16),
            vm((2, NY, FF, T), BF16),
            vm((16, V, C), BF16),
            vm((2, 4, V, C), F32),
            vm((4, V, C), F32),
            vm((3, V, C), I16),
            vm((3, V, C), I16),
            vm((3, 1, C), F32),
            vm((3, 1, C), F32),
            vm((32, 2, C), F32),
            vm((2, D, T // 2), F32),
            vm((2, D, T // 2), I16),
            vm((2, 3, QD, T // 2), I16),
            vm((2, 1, T // 2), F32),
            vm((2, 3, 1, T // 2), F32),
            vm((2, QD, T // 2), I16),
            vm((2, NZ - 1, BD, T // 2), I16),
            vm((2, 1, T // 2), F32),
            vm((2, NZ - 1, 1, T // 2), F32),
            vm((2 * NZ, BD, T), BF16),
            vm((2, V, D), F32),
            vm((NY, FF, QD), F32),
            vm((NY, FF, QD), I16),
            vm((NY, FF, QD), I16),
            vm((1, QD), F32),
            vm((NY, 1, QD), F32),
            vm((8, 8, 128), F32),
            vm((NY, 16, 128), F32),
            vm((NZ, 16, 128), F32),
            vm((8, 2, 128), F32),
            pltpu.SemaphoreType.DMA((3,)),
            pltpu.SemaphoreType.DMA((N_SEM,)),
            pltpu.SemaphoreType.DMA((N_SEM,)),
        ],
        compiler_params=pltpu.CompilerParams(
            collective_id=0, has_side_effects=True, vmem_limit_bytes=56 << 20
        ),
    )(fin, w, hid.T, tgt.reshape(8, C), hro, hco, dro, dco)
    return pl.pallas_call(
        finish,
        out_shape=(
            sds((V, D), F32), sds((V,), F32), sds((D,), F32),
            sds((FF, D), F32), sds((FF,), F32), sds((D,), F32),
        ),
        in_specs=[vmem] * 7,
        out_specs=(vmem,) * 6,
        compiler_params=pltpu.CompilerParams(vmem_limit_bytes=16 << 20),
    )(*raw)


def solution(mesh):
    return jax.shard_map(
        local,
        mesh=mesh,
        in_specs=(
            P("dp", "col"),
            P("row", "col"),
            P("dp", "row"),
            P("dp"),
            P("row"),
            P("col"),
            P("row"),
            P("col"),
        ),
        out_specs=(P("row", "col"), P("row"), P("col"), P("row", "col"), P("row"), P("col")),
        check_vma=False,
    )
```

```python
import jax
import jax.numpy as jnp
from jax import lax
from jax.experimental import pallas as pl
from jax.experimental.pallas import tpu as pltpu
from jax.sharding import PartitionSpec as P

EPS_SQUARE = 1e-30
DECAY_RATE = 1.0 - 10.0 ** (-0.8)
CLIP_LEVEL = 1.0
F32, BF16, I16 = jnp.float32, jnp.bfloat16, jnp.int16
MESH = pl.DeviceIdType.MESH

NZ, NY, NX = 8, 4, 4
T = 1024
V = 512
D = 512
FF = 320
C = 128
FULL_V, FULL_D, FULL_FF = 16384, 4096, 10240
QD = D // NY
BD = QD // NZ
LIMIT = 32766.0
PARTS = ((0, 1), (3, 2))


def tokens_dot(left, right):
    return lax.dot_general(left, right, (((1,), (1,)), ((), ())), preferred_element_type=F32)


def plain_dot(left, right):
    return jnp.dot(left, right, preferred_element_type=F32)


def unit_of(values):
    peak = jnp.max(jnp.abs(values), axis=0, keepdims=True)
    return jnp.maximum(peak, 1e-30) * (1.0 / LIMIT)


def coded(values, unit):
    return jnp.round(values * (1.0 / unit)).astype(jnp.int32).astype(I16)


def decoded(codes, unit):
    return codes.astype(jnp.int32).astype(F32) * unit


def lanes_to_tile(ref, row, vector):
    for part in range(vector.shape[1] // 128):
        ref[pl.ds(row + part, 1), :] = vector[:, 128 * part : 128 * part + 128]


def tile_to_lanes(tile, row, parts):
    return jnp.concatenate([tile[row + p : row + p + 1, :] for p in range(parts)], axis=1)


def column_to_lanes(column):
    return jnp.broadcast_to(column, (column.shape[0], 128)).T[0:1, :]


def lanes_to_column(vector):
    return jnp.broadcast_to(vector, (128, vector.shape[1])).T[:, 0:1]


def body(
    fin_in, w_in, hid_in, tgt, hro, hco, dro, dco,
    hup, hrows, hcols, dup, drows, dcols, clips,
    fin, w, wt, hid, dl,
    both, core_in, x_out, x_in, xu_out, xu_in,
    stat, dft, y_out, y_in, yu_out, yu_in, z_out, z_in, zu_out, zu_in,
    dfb, hg, dq, d_out, d_in, du_out, du_in, htile, rtile, ctile, ztile, stile,
    local_sem, send_sem, recv_sem,
):
    d, row, col = lax.axis_index("dp"), lax.axis_index("row"), lax.axis_index("col")
    z, y, x, k = row // NY, row % NY, col // 2, col % 2
    zz = d * NZ + z
    od = 1 - d

    def at(dd, z_, y_, c_):
        return (dd, z_ * NY + y_, c_)

    def ring(o):
        q = (zz + o) % (2 * NZ)
        return at(q // NZ, q % NZ, y, col)

    def x_peer(o):
        return (d, row, ((x + o) % NX) * 2 + k)

    def y_peer(o):
        return at(d, z, (y + o) % NY, col)

    def z_peer(o):
        return at(d, (z + o) % NZ, y, col)

    core = (d, row, 2 * x + 1 - k)
    dp_peer = (od, row, col)
    mirror = at(od, NZ - 1 - z, y, col)

    pending = []
    count = [0]

    def remote(src, dst, device, slot=None):
        if slot is None:
            slot = count[0]
            count[0] += 1
        copy = pltpu.make_async_remote_copy(
            src_ref=src, dst_ref=dst, send_sem=send_sem.at[slot], recv_sem=recv_sem.at[slot],
            device_id=device, device_id_type=MESH,
        )
        copy.start()
        pending.append(copy)
        return copy

    loads = [
        pltpu.make_async_copy(fin_in, fin.at[pl.ds(d * T, T), :], local_sem.at[0]),
        pltpu.make_async_copy(w_in, w, local_sem.at[1]),
        pltpu.make_async_copy(hid_in, hid.at[d, y], local_sem.at[2]),
    ]
    for load in loads:
        load.start()

    barrier = pltpu.get_barrier_semaphore()

    def greet(device):
        pl.semaphore_signal(barrier, inc=1, device_id=device, device_id_type=MESH)

    @pl.loop(1, 32)
    def _(o):
        greet((d, (row + o) % 32, col))

    @pl.loop(1, 8)
    def _(o):
        greet((d, row, (col + o) % 8))

    others = [dp_peer, mirror] + [ring(o) for o in (1, -1, 2, -2, 4, -4)]
    for device in others:
        greet(device)

    for load in loads:
        load.wait()

    for o in (1, 2, 3, 0):
        start = pl.multiple_of(d * T + ((x + o) % NX) * 2 * C, 2 * C)
        pair = tokens_dot(w[...], fin[pl.ds(start, 2 * C), :])
        both[0, o] = pair[:, 0:C]
        both[1, o] = pair[:, C : 2 * C]
    part = both.at[k]
    wt[...] = w[...].T
    pl.semaphore_wait(barrier, 31 + 7 + len(others))

    core_copies = {}
    for o in (1, 2, 3, 0):
        core_copies[o] = remote(both.at[1 - k, o], core_in.at[o], core)
    fq = pl.ds(pl.multiple_of(d * T + (y * NZ + z) * 32, 32), 32)
    gq = pl.ds(pl.multiple_of(od * T + (y * NZ + NZ - 1 - z) * 32, 32), 32)
    fin_cross = remote(fin.at[fq, :], fin.at[fq, :], mirror)
    hq = pl.ds(pl.multiple_of(col * C, C), C)
    hid_cross = remote(hid.at[d, y, :, hq], hid.at[d, y, :, hq], dp_peer)
    hid_y = [remote(hid.at[d, y], hid.at[d, y], y_peer(o)) for o in (1, 2, 3)]
    x_copies = []
    for o in (1, 2, 3):
        core_copies[o].wait_recv()
        total = part[o] + core_in[o]
        unit = unit_of(total)
        x_out[o - 1] = coded(total, unit)
        xu_out[o - 1] = unit
        x_copies.append(remote(x_out.at[o - 1], x_in.at[o - 1], x_peer(o)))
        x_copies.append(remote(xu_out.at[o - 1], xu_in.at[o - 1], x_peer(o)))
    core_copies[0].wait_recv()
    part[0] = part[0] + core_in[0]
    fin_cross.wait_recv()
    fin_z = [remote(fin.at[gq, :], fin.at[gq, :], z_peer(o)) for o in range(1, NZ)]

    for copy in x_copies:
        copy.wait_recv()
    logits = part[0]
    for o in (1, 2, 3):
        logits = logits + decoded(x_in[o - 1], xu_in[o - 1])
    part[0] = logits

    top = jnp.max(logits, axis=0, keepdims=True)
    total = jnp.sum(jnp.exp(logits - top), axis=0, keepdims=True)
    stat[row, 0:1, :] = top
    stat[row, 1:2, :] = total
    base = count[0]
    count[0] += 31

    def stat_copy(o):
        return pltpu.make_async_remote_copy(
            src_ref=stat.at[row], dst_ref=stat.at[row],
            send_sem=send_sem.at[base + o - 1], recv_sem=recv_sem.at[base + o - 1],
            device_id=(d, (row + o) % 32, col), device_id_type=MESH,
        )

    @pl.loop(1, 32)
    def _(o):
        stat_copy(o).start()

    @pl.loop(1, 32)
    def _(o):
        stat_copy(o).wait_recv()

    stats = stat[...]
    tops, totals = stats[:, 0:1, :], stats[:, 1:2, :]
    row_max = jnp.max(tops, axis=0)
    row_sum = jnp.sum(totals * jnp.exp(tops - row_max[None]), axis=0)
    ids = row * V + lax.broadcasted_iota(jnp.int32, (V, C), 0)
    onehot = (tgt[pl.ds(col, 1), :] == ids).astype(F32)
    dlogits = jnp.exp(part[0] - row_max) / row_sum - onehot
    me = d * 8 + col
    dl[me] = dlogits.astype(BF16)

    def spread_x(half, c):
        slot = half * 8 + c
        first = [remote(dl.at[slot], dl.at[slot], x_peer(o)) for o in (1, 2, 3)]
        return first + [remote(dl.at[slot], dl.at[slot], core)]

    def pass_core(half, copies, o):
        copies[o - 1].wait_recv()
        slot = half * 8 + ((x - o) % NX) * 2 + k
        return remote(dl.at[slot], dl.at[slot], core)

    own_x = spread_x(d, col)
    dl_cross = remote(dl.at[me], dl.at[me], dp_peer)
    own_core = {0: own_x[3]}
    own_core[1] = pass_core(d, own_x, 1)
    own_core[3] = pass_core(d, own_x, 3)
    hid_cross.wait_recv()
    hid_y += [remote(hid.at[od, y, :, hq], hid.at[od, y, :, hq], y_peer(o)) for o in (1, 2, 3)]
    own_core[2] = pass_core(d, own_x, 2)

    y_copies = []
    for p, offsets in enumerate(PARTS):
        for j, o in enumerate(offsets):
            own_core[o].wait_recv()
            for core_ in range(2):
                piece = plain_dot(wt[...], dl[d * 8 + ((x - o) % NX) * 2 + core_])
                unit = unit_of(piece)
                lanes = slice((2 * j + core_) * C, (2 * j + core_ + 1) * C)
                dft[p, :, lanes] = piece
                y_out[p, :, lanes] = coded(piece, unit)
                yu_out[p, :, lanes] = unit
        copies = []
        for o in (1, 2, 3):
            quarter = pl.ds(pl.multiple_of(((y + o) % NY) * QD, QD), QD)
            copies.append(remote(y_out.at[p, quarter, :], y_in.at[p, o - 1], y_peer(o)))
            copies.append(remote(yu_out.at[p], yu_in.at[p, o - 1], y_peer(o)))
        y_copies.append(copies)

    for copy in hid_y:
        copy.wait_recv()
    hid_x = [remote(hid.at[od, :, :, hq], hid.at[od, :, :, hq], x_peer(o)) for o in (1, 2, 3)]
    hid_core = [remote(hid.at[od, :, :, hq], hid.at[od, :, :, hq], core)]

    def head_part(half):
        total = None
        for pair in range(4):
            both = jnp.concatenate([dl[half * 8 + 2 * pair], dl[half * 8 + 2 * pair + 1]], axis=1)
            start = pl.multiple_of(half * T + pair * 2 * C, 2 * C)
            product = plain_dot(both, fin[pl.ds(start, 2 * C), :])
            total = product if total is None else total + product
        return total

    hg[d] = head_part(d)

    z_copies = []
    for p in range(2):
        for copy in y_copies[p]:
            copy.wait_recv()
        quarter = dft[p, pl.ds(pl.multiple_of(y * QD, QD), QD), :]
        for o in (1, 2, 3):
            quarter = quarter + decoded(y_in[p, o - 1], yu_in[p, o - 1])
        dft[p, 0:QD, :] = quarter
        unit = unit_of(quarter)
        zu_out[p] = unit
        z_out[p] = coded(quarter, unit)
        copies = []
        for o in range(1, NZ):
            block = pl.ds(pl.multiple_of(((z + o) % NZ) * BD, BD), BD)
            copies.append(remote(z_out.at[p, block, :], z_in.at[p, o - 1], z_peer(o)))
            copies.append(remote(zu_out.at[p], zu_in.at[p, o - 1], z_peer(o)))
        z_copies.append(copies)

    for copy in fin_z:
        copy.wait_recv()
    gy = pl.ds(pl.multiple_of(od * T + y * 256, 256), 256)
    fin_y = [remote(fin.at[gy, :], fin.at[gy, :], y_peer(o)) for o in (1, 2, 3)]
    dl_cross.wait_recv()
    other_x = spread_x(od, col)

    for p in range(2):
        for copy in z_copies[p]:
            copy.wait_recv()
        block = dft[p, pl.ds(pl.multiple_of(z * BD, BD), BD), :]
        for o in range(1, NZ):
            block = block + decoded(z_in[p, o - 1], zu_in[p, o - 1])
        dfb[zz, :, p * 512 : p * 512 + 512] = block.astype(BF16)

    def block_to(b, device):
        return remote(dfb.at[b], dfb.at[b], device)

    near = {}

    def pass_on(q):
        b = (zz - q) % (2 * NZ)
        for o in (1, -1, 2):
            near[o, q] = block_to(b, ring(o))

    far = {o: block_to(zz, ring(o)) for o in (8, 4, -4)}
    pass_on(0)
    other_core = [other_x[3]] + [pass_core(od, other_x, o) for o in (1, 3, 2)]
    for q in (4, -4, 8):
        far[q].wait_recv()
        pass_on(q)
    for o in (1, 3, 2):
        hid_x[o - 1].wait_recv()
        lanes = pl.ds(pl.multiple_of((((x - o) % NX) * 2 + k) * C, C), C)
        hid_core.append(remote(hid.at[od, :, :, lanes], hid.at[od, :, :, lanes], core))
    for copy in fin_y + other_core:
        copy.wait_recv()
    hg[od] = head_part(od)
    hg[0] = hg[0] + hg[1]
    hsq = hg[0] * hg[0]
    lanes_to_tile(htile.at[col], 0, column_to_lanes(jnp.sum(hsq, axis=1, keepdims=True)))
    head_copies = [
        remote(htile.at[col], htile.at[col], (d, row, (col + o) % 8)) for o in range(1, 8)
    ]
    for copy in near.values():
        copy.wait_recv()
    for copy in hid_core:
        copy.wait_recv()
    total = None
    for half in range(2):
        for p, offsets in enumerate(PARTS):
            for j, o in enumerate(offsets):
                tokens = pl.ds(pl.multiple_of(((x - o) % NX) * 2 * C, 2 * C), 2 * C)
                first = p * 512 + j * 256
                right = dfb[half * NZ : half * NZ + NZ, :, first : first + 256].reshape(QD, 2 * C)
                product = tokens_dot(hid[half, :, :, tokens].reshape(NY * FF, 2 * C), right)
                total = product if total is None else total + product
    dq[...] = total.reshape(NY, FF, QD)
    unit = unit_of(total)
    du_out[...] = unit
    d_out[...] = coded(total, unit).reshape(NY, FF, QD)
    swaps = []
    for o in (1, 2, 3):
        swaps.append(remote(d_out.at[(y + o) % NY], d_in.at[y], y_peer(o)))
        swaps.append(remote(du_out, du_in.at[y], y_peer(o)))
    mine = dq[y]
    d_in[y] = d_out[y]
    du_in[y] = unit
    for copy in head_copies:
        copy.wait_recv()
    hr = DECAY_RATE * hro[...].reshape(1, V) + (1.0 - DECAY_RATE) * (
        tile_to_lanes(jnp.sum(htile[...], axis=0), 0, 4) * (1.0 / FULL_D) + EPS_SQUARE
    )
    hrows[...] = hr
    hr_col = lanes_to_column(hr)
    lanes_to_tile(ctile.at[y], 0, jnp.sum(hsq, axis=0, keepdims=True))
    lanes_to_tile(ctile.at[y], 8, jnp.sum(hsq / hr_col, axis=0, keepdims=True))
    hup[...] = hg[0] * lax.rsqrt(hr_col)
    for copy in swaps:
        copy.wait_recv()
    for q in range(NY):
        dq[q] = decoded(d_in[q], du_in[q])
    dq[y] = mine
    down = jnp.concatenate([dq[q] for q in range(NY)], axis=1)

    rtile[col] = jnp.zeros((4, 128), F32)
    dsq = down * down
    mine = rtile.at[col]
    down_lanes = column_to_lanes(jnp.sum(dsq, axis=1, keepdims=True))
    mine[0:1, :] = down_lanes[:, 0:128]
    mine[1:2, :] = down_lanes[:, 128:256]
    mine[2:3, 0:64] = down_lanes[:, 256:320]
    copies = [remote(rtile.at[col], rtile.at[col], (d, row, (col + o) % 8)) for o in range(1, 8)]
    for copy in copies:
        copy.wait_recv()
    rsum = jnp.sum(rtile[...], axis=0)
    dr = DECAY_RATE * dro[...].reshape(1, FF) + (1.0 - DECAY_RATE) * (
        tile_to_lanes(rsum, 0, 3)[:, 0:FF] * (1.0 / FULL_D) + EPS_SQUARE
    )
    drows[...] = dr
    dr_col = lanes_to_column(dr)

    mine = ctile.at[y]
    lanes_to_tile(mine, 4, jnp.sum(dsq, axis=0, keepdims=True))
    lanes_to_tile(mine, 12, jnp.sum(dsq / dr_col, axis=0, keepdims=True))
    copies = [remote(ctile.at[y], ctile.at[y], y_peer(o)) for o in (1, 2, 3)]
    for copy in copies:
        copy.wait_recv()
    ztile[z] = jnp.sum(ctile[...], axis=0)
    copies = [remote(ztile.at[z], ztile.at[z], z_peer(o)) for o in range(1, NZ)]
    for copy in copies:
        copy.wait_recv()
    csum = jnp.sum(ztile[...], axis=0)
    hc = DECAY_RATE * hco[...].reshape(1, D) + (1.0 - DECAY_RATE) * (
        tile_to_lanes(csum, 0, 4) * (1.0 / FULL_V) + EPS_SQUARE
    )
    dc = DECAY_RATE * dco[...].reshape(1, D) + (1.0 - DECAY_RATE) * (
        tile_to_lanes(csum, 4, 4) * (1.0 / FULL_FF) + EPS_SQUARE
    )
    hcols[...] = hc
    dcols[...] = dc
    hs = jnp.sum(tile_to_lanes(csum, 8, 4) / hc, axis=1, keepdims=True)
    ds = jnp.sum(tile_to_lanes(csum, 12, 4) / dc, axis=1, keepdims=True)
    stile[col, 0:1, :] = jnp.broadcast_to(hs, (1, 128))
    stile[col, 1:2, :] = jnp.broadcast_to(ds, (1, 128))
    copies = [remote(stile.at[col], stile.at[col], (d, row, (col + o) % 8)) for o in range(1, 8)]
    hup[...] = hup[...] * lax.rsqrt(hc)
    dup[...] = down * lax.rsqrt(dr_col) * lax.rsqrt(dc)
    for copy in copies:
        copy.wait_recv()
    clips[...] = jnp.sum(stile[...], axis=0)

    for copy in pending:
        copy.wait_send()

    @pl.loop(1, 32)
    def _(o):
        stat_copy(o).wait_send()


def finish(hraw, hr, hc, draw, dr, dc, squares, hup, hrows, hcols, dup, drows, dcols):
    def clip(square_total, entries):
        return 1.0 / jnp.maximum(1.0, jnp.sqrt(square_total * (1.0 / entries)) / CLIP_LEVEL)

    hup[...] = hraw[...] * clip(squares[0:1, 0:1], FULL_V * FULL_D)
    dup[...] = draw[...] * clip(squares[1:2, 0:1], FULL_FF * FULL_D)
    hrows[...] = hr[...].reshape(V)
    hcols[...] = hc[...].reshape(D)
    drows[...] = dr[...].reshape(FF)
    dcols[...] = dc[...].reshape(D)


N_SEM = 256


def local(fin, w, hid, tgt, hro, hco, dro, dco):
    sds = jax.ShapeDtypeStruct
    vm = pltpu.VMEM
    hbm = pl.BlockSpec(memory_space=pl.ANY)
    vmem = pl.BlockSpec(memory_space=pltpu.VMEM)
    raw = pl.pallas_call(
        body,
        out_shape=(
            sds((V, D), F32), sds((1, V), F32), sds((1, D), F32),
            sds((FF, D), F32), sds((1, FF), F32), sds((1, D), F32), sds((2, 128), F32),
        ),
        in_specs=[hbm] * 3 + [vmem] * 5,
        out_specs=(vmem,) * 7,
        scratch_shapes=[
            vm((2 * T, D), BF16),
            vm((V, D), BF16),
            vm((D, V), BF16),
            vm((2, NY, FF, T), BF16),
            vm((16, V, C), BF16),
            vm((2, 4, V, C), F32),
            vm((4, V, C), F32),
            vm((3, V, C), I16),
            vm((3, V, C), I16),
            vm((3, 1, C), F32),
            vm((3, 1, C), F32),
            vm((32, 2, C), F32),
            vm((2, D, T // 2), F32),
            vm((2, D, T // 2), I16),
            vm((2, 3, QD, T // 2), I16),
            vm((2, 1, T // 2), F32),
            vm((2, 3, 1, T // 2), F32),
            vm((2, QD, T // 2), I16),
            vm((2, NZ - 1, BD, T // 2), I16),
            vm((2, 1, T // 2), F32),
            vm((2, NZ - 1, 1, T // 2), F32),
            vm((2 * NZ, BD, T), BF16),
            vm((2, V, D), F32),
            vm((NY, FF, QD), F32),
            vm((NY, FF, QD), I16),
            vm((NY, FF, QD), I16),
            vm((1, QD), F32),
            vm((NY, 1, QD), F32),
            vm((8, 4, 128), F32),
            vm((8, 4, 128), F32),
            vm((NY, 16, 128), F32),
            vm((NZ, 16, 128), F32),
            vm((8, 2, 128), F32),
            pltpu.SemaphoreType.DMA((3,)),
            pltpu.SemaphoreType.DMA((N_SEM,)),
            pltpu.SemaphoreType.DMA((N_SEM,)),
        ],
        compiler_params=pltpu.CompilerParams(
            collective_id=0, has_side_effects=True, vmem_limit_bytes=56 << 20
        ),
    )(fin, w, hid.T, tgt.reshape(8, C), hro, hco, dro, dco)
    return pl.pallas_call(
        finish,
        out_shape=(
            sds((V, D), F32), sds((V,), F32), sds((D,), F32),
            sds((FF, D), F32), sds((FF,), F32), sds((D,), F32),
        ),
        in_specs=[vmem] * 7,
        out_specs=(vmem,) * 6,
        compiler_params=pltpu.CompilerParams(vmem_limit_bytes=60 << 20),
    )(*raw)


def solution(mesh):
    return jax.shard_map(
        local,
        mesh=mesh,
        in_specs=(
            P("dp", "col"),
            P("row", "col"),
            P("dp", "row"),
            P("dp"),
            P("row"),
            P("col"),
            P("row"),
            P("col"),
        ),
        out_specs=(P("row", "col"), P("row"), P("col"), P("row", "col"), P("row"), P("col")),
        check_vma=False,
    )
```

```python
import jax
import jax.numpy as jnp
from jax import lax
from jax.experimental import pallas as pl
from jax.experimental.pallas import tpu as pltpu
from jax.sharding import PartitionSpec as P

EPS_SQUARE = 1e-30
DECAY_RATE = 1.0 - 10.0 ** (-0.8)
CLIP_LEVEL = 1.0
F32, BF16, I16 = jnp.float32, jnp.bfloat16, jnp.int16
MESH = pl.DeviceIdType.MESH

NZ, NY, NX = 8, 4, 4
T = 1024
V = 512
D = 512
FF = 320
C = 128
FULL_V, FULL_D, FULL_FF = 16384, 4096, 10240
QD = D // NY
BD = QD // NZ
LIMIT = 32766.0
PARTS = ((0, 1), (3, 2))


def tokens_dot(left, right):
    return lax.dot_general(left, right, (((1,), (1,)), ((), ())), preferred_element_type=F32)


def plain_dot(left, right):
    return jnp.dot(left, right, preferred_element_type=F32)


def unit_of(values):
    peak = jnp.max(jnp.abs(values), axis=0, keepdims=True)
    return jnp.maximum(peak, 1e-30) * (1.0 / LIMIT)


def coded(values, unit):
    return jnp.round(values * (1.0 / unit)).astype(jnp.int32).astype(I16)


def decoded(codes, unit):
    return codes.astype(jnp.int32).astype(F32) * unit


def lanes_to_tile(ref, row, vector):
    for part in range(vector.shape[1] // 128):
        ref[pl.ds(row + part, 1), :] = vector[:, 128 * part : 128 * part + 128]


def tile_to_lanes(tile, row, parts):
    return jnp.concatenate([tile[row + p : row + p + 1, :] for p in range(parts)], axis=1)


def column_to_lanes(column):
    return jnp.broadcast_to(column, (column.shape[0], 128)).T[0:1, :]


def lanes_to_column(vector):
    return jnp.broadcast_to(vector, (128, vector.shape[1])).T[:, 0:1]


def body(
    fin_in, w_in, hid_in, tgt, hro, hco, dro, dco,
    hup, hrows, hcols, dup, drows, dcols, clips,
    fin, w, wt, hid, dl,
    both, core_in, x_out, x_in, xu_out, xu_in,
    stat, dft, y_out, y_in, yu_out, yu_in, z_out, z_in, zu_out, zu_in,
    dfb, hg, dq, d_out, d_in, du_out, du_in, htile, rtile, ctile, ztile, stile,
    local_sem, send_sem, recv_sem,
):
    d, row, col = lax.axis_index("dp"), lax.axis_index("row"), lax.axis_index("col")
    z, y, x, k = row // NY, row % NY, col // 2, col % 2
    zz = d * NZ + z
    od = 1 - d

    def at(dd, z_, y_, c_):
        return (dd, z_ * NY + y_, c_)

    def ring(o):
        q = (zz + o) % (2 * NZ)
        return at(q // NZ, q % NZ, y, col)

    def x_peer(o):
        return (d, row, ((x + o) % NX) * 2 + k)

    def y_peer(o):
        return at(d, z, (y + o) % NY, col)

    def z_peer(o):
        return at(d, (z + o) % NZ, y, col)

    core = (d, row, 2 * x + 1 - k)
    dp_peer = (od, row, col)
    mirror = at(od, NZ - 1 - z, y, col)

    pending = []
    count = [0]

    def remote(src, dst, device, slot=None):
        if slot is None:
            slot = count[0]
            count[0] += 1
        copy = pltpu.make_async_remote_copy(
            src_ref=src, dst_ref=dst, send_sem=send_sem.at[slot], recv_sem=recv_sem.at[slot],
            device_id=device, device_id_type=MESH,
        )
        copy.start()
        pending.append(copy)
        return copy

    loads = [
        pltpu.make_async_copy(fin_in, fin.at[pl.ds(d * T, T), :], local_sem.at[0]),
        pltpu.make_async_copy(w_in, w, local_sem.at[1]),
        pltpu.make_async_copy(hid_in, hid.at[d, y], local_sem.at[2]),
    ]
    for load in loads:
        load.start()

    barrier = pltpu.get_barrier_semaphore()

    def greet(device):
        pl.semaphore_signal(barrier, inc=1, device_id=device, device_id_type=MESH)

    others = [dp_peer, mirror] + [ring(o) for o in (4, -4, 2, -2, 1, -1)]
    for device in others:
        greet(device)

    @pl.loop(0, 31)
    def _(o):
        greet((d, (row + 1 + (o + 12) % 31) % 32, col))

    @pl.loop(1, 8)
    def _(o):
        greet((d, row, (col + o) % 8))

    loads[0].wait()
    loads[1].wait()

    for o in (1, 2, 3, 0):
        start = pl.multiple_of(d * T + ((x + o) % NX) * 2 * C, 2 * C)
        pair = tokens_dot(w[...], fin[pl.ds(start, 2 * C), :])
        both[0, o] = pair[:, 0:C]
        both[1, o] = pair[:, C : 2 * C]
    part = both.at[k]
    loads[2].wait()
    pl.semaphore_wait(barrier, 31 + 7 + len(others))

    core_copies = {}
    for o in (1, 2, 3, 0):
        core_copies[o] = remote(both.at[1 - k, o], core_in.at[o], core)
    fq = pl.ds(pl.multiple_of(d * T + (y * NZ + z) * 32, 32), 32)
    gq = pl.ds(pl.multiple_of(od * T + (y * NZ + NZ - 1 - z) * 32, 32), 32)
    fin_cross = remote(fin.at[fq, :], fin.at[fq, :], mirror)
    hq = pl.ds(pl.multiple_of(col * C, C), C)
    hid_cross = remote(hid.at[d, y, :, hq], hid.at[d, y, :, hq], dp_peer)
    hid_y = [remote(hid.at[d, y], hid.at[d, y], y_peer(o)) for o in (1, 2, 3)]
    wt[...] = w[...].T
    x_copies = []
    for o in (1, 2, 3):
        core_copies[o].wait_recv()
        total = part[o] + core_in[o]
        unit = unit_of(total)
        x_out[o - 1] = coded(total, unit)
        xu_out[o - 1] = unit
        x_copies.append(remote(x_out.at[o - 1], x_in.at[o - 1], x_peer(o)))
        x_copies.append(remote(xu_out.at[o - 1], xu_in.at[o - 1], x_peer(o)))
    core_copies[0].wait_recv()
    part[0] = part[0] + core_in[0]
    fin_cross.wait_recv()
    fin_z = [remote(fin.at[gq, :], fin.at[gq, :], z_peer(o)) for o in range(1, NZ)]

    for copy in x_copies:
        copy.wait_recv()
    logits = part[0]
    for o in (1, 2, 3):
        logits = logits + decoded(x_in[o - 1], xu_in[o - 1])
    part[0] = logits

    top = jnp.max(logits, axis=0, keepdims=True)
    total = jnp.sum(jnp.exp(logits - top), axis=0, keepdims=True)
    stat[row, 0:1, :] = top
    stat[row, 1:2, :] = total
    base = count[0]
    count[0] += 31

    def stat_copy(o):
        return pltpu.make_async_remote_copy(
            src_ref=stat.at[row], dst_ref=stat.at[row],
            send_sem=send_sem.at[base + o - 1], recv_sem=recv_sem.at[base + o - 1],
            device_id=(d, (row + o) % 32, col), device_id_type=MESH,
        )

    @pl.loop(1, 32)
    def _(o):
        stat_copy(o).start()

    @pl.loop(1, 32)
    def _(o):
        stat_copy(o).wait_recv()

    stats = stat[...]
    tops, totals = stats[:, 0:1, :], stats[:, 1:2, :]
    row_max = jnp.max(tops, axis=0)
    row_sum = jnp.sum(totals * jnp.exp(tops - row_max[None]), axis=0)
    ids = row * V + lax.broadcasted_iota(jnp.int32, (V, C), 0)
    onehot = (tgt[pl.ds(col, 1), :] == ids).astype(F32)
    dlogits = jnp.exp(part[0] - row_max) / row_sum - onehot
    me = d * 8 + col
    dl[me] = dlogits.astype(BF16)

    def spread_x(half, c):
        slot = half * 8 + c
        first = [remote(dl.at[slot], dl.at[slot], x_peer(o)) for o in (1, 2, 3)]
        return first + [remote(dl.at[slot], dl.at[slot], core)]

    def pass_core(half, copies, o):
        copies[o - 1].wait_recv()
        slot = half * 8 + ((x - o) % NX) * 2 + k
        return remote(dl.at[slot], dl.at[slot], core)

    own_x = spread_x(d, col)
    dl_cross = remote(dl.at[me], dl.at[me], dp_peer)
    own_core = {0: own_x[3]}
    own_core[1] = pass_core(d, own_x, 1)
    own_core[3] = pass_core(d, own_x, 3)
    hid_cross.wait_recv()
    hid_y += [remote(hid.at[od, y, :, hq], hid.at[od, y, :, hq], y_peer(o)) for o in (1, 2, 3)]
    own_core[2] = pass_core(d, own_x, 2)

    y_copies = []
    for p, offsets in enumerate(PARTS):
        for j, o in enumerate(offsets):
            own_core[o].wait_recv()
            for core_ in range(2):
                piece = plain_dot(wt[...], dl[d * 8 + ((x - o) % NX) * 2 + core_])
                unit = unit_of(piece)
                lanes = slice((2 * j + core_) * C, (2 * j + core_ + 1) * C)
                dft[p, :, lanes] = piece
                y_out[p, :, lanes] = coded(piece, unit)
                yu_out[p, :, lanes] = unit
        copies = []
        for o in (1, 2, 3):
            quarter = pl.ds(pl.multiple_of(((y + o) % NY) * QD, QD), QD)
            copies.append(remote(y_out.at[p, quarter, :], y_in.at[p, o - 1], y_peer(o)))
            copies.append(remote(yu_out.at[p], yu_in.at[p, o - 1], y_peer(o)))
        y_copies.append(copies)

    for copy in hid_y:
        copy.wait_recv()
    hid_x = [remote(hid.at[od, :, :, hq], hid.at[od, :, :, hq], x_peer(o)) for o in (1, 2, 3)]
    hid_core = [remote(hid.at[od, :, :, hq], hid.at[od, :, :, hq], core)]

    def head_part(half):
        total = None
        for pair in range(4):
            both = jnp.concatenate([dl[half * 8 + 2 * pair], dl[half * 8 + 2 * pair + 1]], axis=1)
            start = pl.multiple_of(half * T + pair * 2 * C, 2 * C)
            product = plain_dot(both, fin[pl.ds(start, 2 * C), :])
            total = product if total is None else total + product
        return total

    z_copies = []
    for p in range(2):
        for copy in y_copies[p]:
            copy.wait_recv()
        quarter = dft[p, pl.ds(pl.multiple_of(y * QD, QD), QD), :]
        for o in (1, 2, 3):
            quarter = quarter + decoded(y_in[p, o - 1], yu_in[p, o - 1])
        dft[p, 0:QD, :] = quarter
        unit = unit_of(quarter)
        zu_out[p] = unit
        z_out[p] = coded(quarter, unit)
        copies = []
        for o in range(1, NZ):
            block = pl.ds(pl.multiple_of(((z + o) % NZ) * BD, BD), BD)
            copies.append(remote(z_out.at[p, block, :], z_in.at[p, o - 1], z_peer(o)))
            copies.append(remote(zu_out.at[p], zu_in.at[p, o - 1], z_peer(o)))
        z_copies.append(copies)

    for copy in fin_z:
        copy.wait_recv()
    gy = pl.ds(pl.multiple_of(od * T + y * 256, 256), 256)
    fin_y = [remote(fin.at[gy, :], fin.at[gy, :], y_peer(o)) for o in (1, 2, 3)]
    dl_cross.wait_recv()
    other_x = spread_x(od, col)
    hg[d] = head_part(d)

    for p in range(2):
        for copy in z_copies[p]:
            copy.wait_recv()
        block = dft[p, pl.ds(pl.multiple_of(z * BD, BD), BD), :]
        for o in range(1, NZ):
            block = block + decoded(z_in[p, o - 1], zu_in[p, o - 1])
        dfb[zz, :, p * 512 : p * 512 + 512] = block.astype(BF16)

    def block_to(b, device):
        return remote(dfb.at[b], dfb.at[b], device)

    near = {}

    def pass_on(q):
        b = (zz - q) % (2 * NZ)
        for o in (1, -1, 2):
            near[o, q] = block_to(b, ring(o))

    far = {o: block_to(zz, ring(o)) for o in (8, 4, -4)}
    pass_on(0)
    other_core = [other_x[3]] + [pass_core(od, other_x, o) for o in (1, 3, 2)]
    for q in (4, -4, 8):
        far[q].wait_recv()
        pass_on(q)
    for o in (1, 3, 2):
        hid_x[o - 1].wait_recv()
        lanes = pl.ds(pl.multiple_of((((x - o) % NX) * 2 + k) * C, C), C)
        hid_core.append(remote(hid.at[od, :, :, lanes], hid.at[od, :, :, lanes], core))
    for copy in fin_y + other_core:
        copy.wait_recv()
    hg[od] = head_part(od)
    hg[0] = hg[0] + hg[1]
    hsq = hg[0] * hg[0]
    lanes_to_tile(htile.at[col], 0, column_to_lanes(jnp.sum(hsq, axis=1, keepdims=True)))
    head_copies = [
        remote(htile.at[col], htile.at[col], (d, row, (col + o) % 8)) for o in range(1, 8)
    ]
    for copy in near.values():
        copy.wait_recv()
    for copy in hid_core:
        copy.wait_recv()
    total = None
    for half in range(2):
        for p, offsets in enumerate(PARTS):
            for j, o in enumerate(offsets):
                tokens = pl.ds(pl.multiple_of(((x - o) % NX) * 2 * C, 2 * C), 2 * C)
                first = p * 512 + j * 256
                right = dfb[half * NZ : half * NZ + NZ, :, first : first + 256].reshape(QD, 2 * C)
                product = tokens_dot(hid[half, :, :, tokens].reshape(NY * FF, 2 * C), right)
                total = product if total is None else total + product
    dq[...] = total.reshape(NY, FF, QD)
    unit = unit_of(total)
    du_out[...] = unit
    d_out[...] = coded(total, unit).reshape(NY, FF, QD)
    swaps = []
    for o in (1, 2, 3):
        swaps.append(remote(d_out.at[(y + o) % NY], d_in.at[y], y_peer(o)))
        swaps.append(remote(du_out, du_in.at[y], y_peer(o)))
    mine = dq[y]
    d_in[y] = d_out[y]
    du_in[y] = unit
    for copy in head_copies:
        copy.wait_recv()
    hr = DECAY_RATE * hro[...].reshape(1, V) + (1.0 - DECAY_RATE) * (
        tile_to_lanes(jnp.sum(htile[...], axis=0), 0, 4) * (1.0 / FULL_D) + EPS_SQUARE
    )
    hrows[...] = hr
    hr_col = lanes_to_column(hr)
    lanes_to_tile(ctile.at[y], 0, jnp.sum(hsq, axis=0, keepdims=True))
    lanes_to_tile(ctile.at[y], 8, jnp.sum(hsq / hr_col, axis=0, keepdims=True))
    hup[...] = hg[0] * lax.rsqrt(hr_col)
    for copy in swaps:
        copy.wait_recv()
    for q in range(NY):
        dq[q] = decoded(d_in[q], du_in[q])
    dq[y] = mine
    down = jnp.concatenate([dq[q] for q in range(NY)], axis=1)

    rtile[col] = jnp.zeros((4, 128), F32)
    dsq = down * down
    mine = rtile.at[col]
    down_lanes = column_to_lanes(jnp.sum(dsq, axis=1, keepdims=True))
    mine[0:1, :] = down_lanes[:, 0:128]
    mine[1:2, :] = down_lanes[:, 128:256]
    mine[2:3, 0:64] = down_lanes[:, 256:320]
    copies = [remote(rtile.at[col], rtile.at[col], (d, row, (col + o) % 8)) for o in range(1, 8)]
    for copy in copies:
        copy.wait_recv()
    rsum = jnp.sum(rtile[...], axis=0)
    dr = DECAY_RATE * dro[...].reshape(1, FF) + (1.0 - DECAY_RATE) * (
        tile_to_lanes(rsum, 0, 3)[:, 0:FF] * (1.0 / FULL_D) + EPS_SQUARE
    )
    drows[...] = dr
    dr_col = lanes_to_column(dr)

    mine = ctile.at[y]
    lanes_to_tile(mine, 4, jnp.sum(dsq, axis=0, keepdims=True))
    lanes_to_tile(mine, 12, jnp.sum(dsq / dr_col, axis=0, keepdims=True))
    copies = [remote(ctile.at[y], ctile.at[y], y_peer(o)) for o in (1, 2, 3)]
    for copy in copies:
        copy.wait_recv()
    ztile[z] = jnp.sum(ctile[...], axis=0)
    copies = [remote(ztile.at[z], ztile.at[z], z_peer(o)) for o in range(1, NZ)]
    for copy in copies:
        copy.wait_recv()
    csum = jnp.sum(ztile[...], axis=0)
    hc = DECAY_RATE * hco[...].reshape(1, D) + (1.0 - DECAY_RATE) * (
        tile_to_lanes(csum, 0, 4) * (1.0 / FULL_V) + EPS_SQUARE
    )
    dc = DECAY_RATE * dco[...].reshape(1, D) + (1.0 - DECAY_RATE) * (
        tile_to_lanes(csum, 4, 4) * (1.0 / FULL_FF) + EPS_SQUARE
    )
    hcols[...] = hc
    dcols[...] = dc
    hs = jnp.sum(tile_to_lanes(csum, 8, 4) / hc, axis=1, keepdims=True)
    ds = jnp.sum(tile_to_lanes(csum, 12, 4) / dc, axis=1, keepdims=True)
    stile[col, 0:1, :] = jnp.broadcast_to(hs, (1, 128))
    stile[col, 1:2, :] = jnp.broadcast_to(ds, (1, 128))
    copies = [remote(stile.at[col], stile.at[col], (d, row, (col + o) % 8)) for o in range(1, 8)]
    hup[...] = hup[...] * lax.rsqrt(hc)
    dup[...] = down * lax.rsqrt(dr_col) * lax.rsqrt(dc)
    for copy in copies:
        copy.wait_recv()
    clips[...] = jnp.sum(stile[...], axis=0)

    for copy in pending:
        copy.wait_send()

    @pl.loop(1, 32)
    def _(o):
        stat_copy(o).wait_send()


def finish(hraw, hr, hc, draw, dr, dc, squares, hup, hrows, hcols, dup, drows, dcols):
    def clip(square_total, entries):
        return 1.0 / jnp.maximum(1.0, jnp.sqrt(square_total * (1.0 / entries)) / CLIP_LEVEL)

    hup[...] = hraw[...] * clip(squares[0:1, 0:1], FULL_V * FULL_D)
    dup[...] = draw[...] * clip(squares[1:2, 0:1], FULL_FF * FULL_D)
    hrows[...] = hr[...].reshape(V)
    hcols[...] = hc[...].reshape(D)
    drows[...] = dr[...].reshape(FF)
    dcols[...] = dc[...].reshape(D)


N_SEM = 256


def local(fin, w, hid, tgt, hro, hco, dro, dco):
    sds = jax.ShapeDtypeStruct
    vm = pltpu.VMEM
    hbm = pl.BlockSpec(memory_space=pl.ANY)
    vmem = pl.BlockSpec(memory_space=pltpu.VMEM)
    raw = pl.pallas_call(
        body,
        out_shape=(
            sds((V, D), F32), sds((1, V), F32), sds((1, D), F32),
            sds((FF, D), F32), sds((1, FF), F32), sds((1, D), F32), sds((2, 128), F32),
        ),
        in_specs=[hbm] * 3 + [vmem] * 5,
        out_specs=(vmem,) * 7,
        scratch_shapes=[
            vm((2 * T, D), BF16),
            vm((V, D), BF16),
            vm((D, V), BF16),
            vm((2, NY, FF, T), BF16),
            vm((16, V, C), BF16),
            vm((2, 4, V, C), F32),
            vm((4, V, C), F32),
            vm((3, V, C), I16),
            vm((3, V, C), I16),
            vm((3, 1, C), F32),
            vm((3, 1, C), F32),
            vm((32, 2, C), F32),
            vm((2, D, T // 2), F32),
            vm((2, D, T // 2), I16),
            vm((2, 3, QD, T // 2), I16),
            vm((2, 1, T // 2), F32),
            vm((2, 3, 1, T // 2), F32),
            vm((2, QD, T // 2), I16),
            vm((2, NZ - 1, BD, T // 2), I16),
            vm((2, 1, T // 2), F32),
            vm((2, NZ - 1, 1, T // 2), F32),
            vm((2 * NZ, BD, T), BF16),
            vm((2, V, D), F32),
            vm((NY, FF, QD), F32),
            vm((NY, FF, QD), I16),
            vm((NY, FF, QD), I16),
            vm((1, QD), F32),
            vm((NY, 1, QD), F32),
            vm((8, 4, 128), F32),
            vm((8, 4, 128), F32),
            vm((NY, 16, 128), F32),
            vm((NZ, 16, 128), F32),
            vm((8, 2, 128), F32),
            pltpu.SemaphoreType.DMA((3,)),
            pltpu.SemaphoreType.DMA((N_SEM,)),
            pltpu.SemaphoreType.DMA((N_SEM,)),
        ],
        compiler_params=pltpu.CompilerParams(
            collective_id=0, has_side_effects=True, vmem_limit_bytes=56 << 20
        ),
    )(fin, w, hid.T, tgt.reshape(8, C), hro, hco, dro, dco)
    return pl.pallas_call(
        finish,
        out_shape=(
            sds((V, D), F32), sds((V,), F32), sds((D,), F32),
            sds((FF, D), F32), sds((FF,), F32), sds((D,), F32),
        ),
        in_specs=[vmem] * 7,
        out_specs=(vmem,) * 6,
        compiler_params=pltpu.CompilerParams(vmem_limit_bytes=60 << 20),
    )(*raw)


def solution(mesh):
    return jax.shard_map(
        local,
        mesh=mesh,
        in_specs=(
            P("dp", "col"),
            P("row", "col"),
            P("dp", "row"),
            P("dp"),
            P("row"),
            P("col"),
            P("row"),
            P("col"),
        ),
        out_specs=(P("row", "col"), P("row"), P("col"), P("row", "col"), P("row"), P("col")),
        check_vma=False,
    )
```
